128 devices in a mesh: shot: 16 (over z_hi, x, core), slab: 8 (over y, z_lo).
Axes of the slice: x: 4, y: 4, z: 4 (z_hi: 2, z_lo: 2; z = z_hi * 2 + z_lo), core: 2. Of those that a mesh axis runs over, the one named last changes fastest.
Arguments:
- kappa: float32 [128, 256, 256], P('slab', 'shot'), may hold values from 0.05 to 0.25
- buoyancy: float32 [128, 256, 256], P('slab', 'shot'), may hold values from 0.5 to 1
- anchors: int32 [16, 2], replicated, may hold values from 0 to 128
- wave_start: float32 [16, 2, 128, 128, 128], P('shot', None, 'slab'), may hold values from -1.8 to 1.8
- adjoint_start: float32 [16, 2, 128, 128, 128], P('shot', None, 'slab'), may hold values from -1.8 to 1.8
- wavelet: float32 [16, 4], P('shot'), may hold values from -4 to 4
- source_cell: int32 [16, 3], P('shot'), may hold values from 0 to 127
- receiver_cells: int32 [16, 512, 3], P('shot'), may hold values from 0 to 127
- observed: float32 [16, 4, 512], P('shot'), may hold values from -3 to 3
Outputs:
- model_grad: float32 [128, 256, 256], P('slab', 'shot')
- wave_end: float32 [16, 2, 128, 128, 128], P('shot', None, 'slab')
- adjoint_end: float32 [16, 2, 128, 128, 128], P('shot', None, 'slab')
The draws below stay inside these ranges and needn't reach their ends.
Inputs may be any that keep to these rules, and one draw needn't show every extreme that they name: `anchors`: apertures lie inside the model; several shots' apertures may cover the same cells. `receiver_cells`: several receivers may share a cell.
All inputs are finite; a program needn't handle non-finite values.
Results may differ from the reference program's by a relative error of at most 0.00002.
Values sent between devices are 32-bit elements; how exact they have to be, the bound alone decides.
A program may use at most 128 MiB of HBM per device.

```python
import math
import jax
import jax.numpy as jnp
from jax import lax

AP = 128
NT = 4
NREC = 512
SHOTS = 16
M = 256
NZ = 128


def touch_ends(array, stream_key, least, high):
    shape = array.shape
    index_at = [jax.random.randint(jax.random.fold_in(stream_key, axis), (), 0, shape[axis]) for axis in range(len(shape))]
    array = array.at[tuple(index_at)].set(least)
    longest = shape.index(max(shape))
    index_at[longest] = (index_at[longest] + 1) % shape[longest]
    return array.at[tuple(index_at)].set(high)


def shard_levels(stream_key, shape, pieces, least, largest):
    def one(axis_at, shards_of):
        heights = jax.random.uniform(jax.random.fold_in(jax.random.fold_in(stream_key, 6), axis_at), (shards_of,), jnp.float32, least / len(pieces), largest / len(pieces))
        return jnp.repeat(jnp.exp(heights), shape[axis_at] // shards_of).reshape((-1,) + (1,) * (len(shape) - axis_at - 1))

    factor_of = one(*pieces[0])
    for cut in pieces[1:]:
        factor_of = factor_of * one(*cut)
    return factor_of


def centred(stream_key, extent, scale, limit, pieces=(), kind=jnp.bfloat16):
    values = jax.random.normal(stream_key, extent, jnp.float32) * scale
    if len(pieces) > 0:
        values = shard_levels(stream_key, extent, pieces, -0.22, 0.18) * values
    return jnp.clip(values, min=-limit, max=limit).astype(kind)


def setup_inputs(seed: int = 0) -> dict:
    key_of = jax.random.split(jax.random.key(seed), 10)
    kappa = jnp.clip(jnp.exp(math.log(0.25) - 1.609438 * jax.random.uniform(key_of[0], (NZ, M, M), jnp.float32) ** shard_levels(key_of[0], (NZ, M, M), ((0, 8), (1, 16)), -0.2, 0.2)), 0.05, 0.25)
    buoyancy = jnp.clip(0.5 + 0.5 * jax.random.uniform(key_of[1], (NZ, M, M), jnp.float32) ** shard_levels(key_of[1], (NZ, M, M), ((0, 8), (1, 16)), -0.2, 0.2), 0.5, 1.0)
    anchors = touch_ends(jax.random.randint(key_of[2], (SHOTS, 2), 0, M - AP + 1), jax.random.fold_in(key_of[2], 1), 0, M - AP).astype(jnp.int32)
    wave_start = centred(key_of[3], (SHOTS, 2, NZ, AP, AP), 0.3, 1.8, ((0, 16), (2, 8)), jnp.float32)
    adjoint_start = centred(key_of[4], (SHOTS, 2, NZ, AP, AP), 0.3, 1.8, ((0, 16), (2, 8)), jnp.float32)
    wavelet = centred(key_of[5], (SHOTS, NT), 1.0, 4.0, ((0, 16),), jnp.float32)
    source_cell = touch_ends(jax.random.randint(key_of[6], (SHOTS, 3), 0, AP), jax.random.fold_in(key_of[6], 1), 0, AP - 1).astype(jnp.int32)
    receiver_cells = touch_ends(jax.random.randint(key_of[7], (SHOTS, NREC, 3), 0, AP), jax.random.fold_in(key_of[7], 1), 0, AP - 1).astype(jnp.int32)
    observed = centred(key_of[8], (SHOTS, NT, NREC), 0.5, 3.0, ((0, 16),), jnp.float32)
    return dict(kappa=kappa, buoyancy=buoyancy, anchors=anchors, wave_start=wave_start, adjoint_start=adjoint_start, wavelet=wavelet, source_cell=source_cell, receiver_cells=receiver_cells, observed=observed)


def faces_of(buoy):
    pad_depth = jnp.pad(buoy, ((1, 1), (0, 0), (0, 0)))
    pad_rows = jnp.pad(buoy, ((0, 0), (1, 1), (0, 0)))
    pad_cols = jnp.pad(buoy, ((0, 0), (0, 0), (1, 1)))
    depth_face = 0.5 * (pad_depth[1:] + pad_depth[:-1])
    row_face = 0.5 * (pad_rows[:, 1:] + pad_rows[:, :-1])
    col_face = 0.5 * (pad_cols[:, :, 1:] + pad_cols[:, :, :-1])
    return depth_face, row_face, col_face


def spread_of(field, faces):
    depth_face, row_face, col_face = faces
    pad_depth = jnp.pad(field, ((1, 1), (0, 0), (0, 0)))
    flux = depth_face * (pad_depth[1:] - pad_depth[:-1])
    result = flux[1:] - flux[:-1]
    pad_rows = jnp.pad(field, ((0, 0), (1, 1), (0, 0)))
    flux = row_face * (pad_rows[:, 1:] - pad_rows[:, :-1])
    result = result + (flux[:, 1:] - flux[:, :-1])
    pad_cols = jnp.pad(field, ((0, 0), (0, 0), (1, 1)))
    flux = col_face * (pad_cols[:, :, 1:] - pad_cols[:, :, :-1])
    return result + (flux[:, :, 1:] - flux[:, :, :-1])


def reference(kappa, buoyancy, anchors, wave_start, adjoint_start, wavelet, source_cell, receiver_cells, observed):
    def one_shot(total, inputs):
        anchor, wave, adjoint, pulse, source, receivers, observed_shot = inputs
        zero_index = anchor[0] * 0
        kappa_window = lax.dynamic_slice(kappa, (zero_index, anchor[0], anchor[1]), (NZ, AP, AP))
        buoy_window = lax.dynamic_slice(buoyancy, (zero_index, anchor[0], anchor[1]), (NZ, AP, AP))
        faces = faces_of(buoy_window)
        before = wave[0]
        current = wave[1]
        spreads = []
        residuals = []
        for moment in range(NT):
            spread = spread_of(current, faces)
            spreads.append(spread)
            following = 2.0 * current - before + kappa_window * spread
            following = following.at[source[0], source[1], source[2]].add(pulse[moment])
            sampled = following[receivers[:, 0], receivers[:, 1], receivers[:, 2]]
            residuals.append(sampled - observed_shot[moment])
            before = current
            current = following
        after = adjoint[0]
        later = adjoint[1]
        imaging = None
        for moment in reversed(range(NT)):
            adjoint_now = 2.0 * later - after + spread_of(kappa_window * later, faces)
            adjoint_now = adjoint_now.at[receivers[:, 0], receivers[:, 1], receivers[:, 2]].add(residuals[moment])
            term = adjoint_now * spreads[moment]
            imaging = term if imaging is None else imaging + term
            after = later
            later = adjoint_now
        region = lax.dynamic_slice(total, (zero_index, anchor[0], anchor[1]), (NZ, AP, AP))
        total = lax.dynamic_update_slice(total, region + imaging, (zero_index, anchor[0], anchor[1]))
        return total, (jnp.stack([before, current]), jnp.stack([after, later]))

    start = jnp.zeros((NZ, M, M), jnp.float32)
    inputs = (anchors, wave_start, adjoint_start, wavelet, source_cell, receiver_cells, observed)
    total, outputs = lax.scan(one_shot, start, inputs)
    return total, outputs[0], outputs[1]
```

```python
import functools

import jax
import jax.numpy as jnp
from jax import lax
from jax.experimental import pallas as pl
from jax.experimental.pallas import tpu as pltpu
from jax.sharding import PartitionSpec as P

MESH = pl.DeviceIdType.MESH
NT = 4
PAD = 8
CHUNK = 32
OFFSETS = ((2, 0), (2, 1), (1, 0), (3, 0), (1, 1), (3, 1), (0, 1))


def kernel(
    anchors,
    wavelet,
    source,
    kappa,
    buoyancy,
    wave,
    adjoint,
    cells,
    observed,
    grad_out,
    wave_out,
    adjoint_out,
    raw,
    pack,
    win,
    pb,
    pm,
    qb,
    kp,
    bz,
    fd,
    cr,
    cc,
    dg,
    wb,
    ab,
    kc,
    ob,
    sf,
    vb,
    gb,
    gc,
    gr,
    acc,
    pr,
    tmp,
    load_sem,
    swap_send,
    swap_recv,
    win_send,
    win_recv,
    halo_send,
    halo_recv,
    grad_send,
    grad_recv,
    out_sem,
):
    depth, own, side = kappa.shape
    ap = side // 2
    f32 = jnp.float32
    shot = lax.axis_index("shot")
    slab = lax.axis_index("slab")
    slabs = lax.axis_size("slab")
    half = shot // 8
    lane_group = shot % 8
    px = lane_group // 2
    pc = lane_group % 2
    partner = (shot + 8) % 16
    below = (slab + 1) % slabs
    above = (slab + slabs - 1) % slabs

    def peer(o):
        dx, dc = OFFSETS[o]
        return ((px + dx) % 4) * 2 + (pc + dc) % 2

    def origin(o):
        dx, dc = OFFSETS[o]
        return ((px + 4 - dx) % 4) * 2 + (pc + dc) % 2

    inner = pl.ds(PAD, ap)
    body = pl.ds(1, depth)
    loads = [
        pltpu.make_async_copy(buoyancy, raw.at[half, 0], load_sem.at[0]),
        pltpu.make_async_copy(kappa, raw.at[half, 1], load_sem.at[1]),
        pltpu.make_async_copy(wave.at[0, 1], pb.at[0, body, inner, :], load_sem.at[2]),
        pltpu.make_async_copy(wave.at[0, 0], pm, load_sem.at[3]),
        pltpu.make_async_copy(adjoint.at[0, 1], ab.at[1], load_sem.at[4]),
        pltpu.make_async_copy(adjoint.at[0, 0], ab.at[0], load_sem.at[5]),
    ]
    for copy in loads:
        copy.start()

    barrier = pltpu.get_barrier_semaphore()
    pl.semaphore_signal(barrier, inc=1, device_id={"shot": partner, "slab": slab}, device_id_type=MESH)
    pl.semaphore_signal(barrier, inc=1, device_id={"shot": shot, "slab": below}, device_id_type=MESH)
    pl.semaphore_signal(barrier, inc=1, device_id={"shot": shot, "slab": above}, device_id_type=MESH)
    for o in range(7):
        pl.semaphore_signal(
            barrier, inc=1, device_id={"shot": half * 8 + peer(o), "slab": slab}, device_id_type=MESH
        )
    pl.semaphore_wait(barrier, 10)

    swaps = []
    for i, ref in enumerate((buoyancy, kappa)):
        swaps.append(
            pltpu.make_async_remote_copy(
                src_ref=ref,
                dst_ref=raw.at[half, i],
                send_sem=swap_send.at[i],
                recv_sem=swap_recv.at[i],
                device_id={"shot": partner, "slab": slab},
                device_id_type=MESH,
            )
        )
        swaps[-1].start()

    def halo_pair(slot, first, last, low, high):
        up = pltpu.make_async_remote_copy(
            src_ref=first,
            dst_ref=high,
            send_sem=halo_send.at[slot, 0],
            recv_sem=halo_recv.at[slot, 0],
            device_id={"shot": shot, "slab": above},
            device_id_type=MESH,
        )
        down = pltpu.make_async_remote_copy(
            src_ref=last,
            dst_ref=low,
            send_sem=halo_send.at[slot, 1],
            recv_sem=halo_recv.at[slot, 1],
            device_id={"shot": shot, "slab": below},
            device_id_type=MESH,
        )
        return (up, down)

    def field_halo(slot, field, src=None):
        first = field.at[1, inner, :] if src is None else src.at[0]
        last = field.at[depth, inner, :] if src is None else src.at[depth - 1]
        return halo_pair(
            slot, first, last, field.at[0, inner, :], field.at[depth + 1, inner, :]
        )

    halos = [field_halo(0, pb.at[0], wave.at[0, 1])]
    halos += [field_halo(n, pb.at[n]) for n in range(1, NT)]
    halos += [field_halo(NT + m, wb.at[m]) for m in range(NT)]
    halos.append(field_halo(2 * NT, bz))

    def go(pair):
        pair[0].start()
        pair[1].start()

    def arrived(pair):
        pair[0].wait_recv()
        pair[1].wait_recv()

    go(halos[0])

    margin = jnp.zeros((PAD, ap), f32)

    def clear(i, carry):
        for n in range(NT):
            pb[n, i + 1, :PAD, :] = margin
            pb[n, i + 1, PAD + ap :, :] = margin
            wb[n, i + 1, :PAD, :] = margin
            wb[n, i + 1, PAD + ap :, :] = margin
        bz[i + 1, :PAD, :] = margin
        bz[i + 1, PAD + ap :, :] = margin
        cr[i, PAD + ap :, :] = margin
        return carry

    lax.fori_loop(0, depth, clear, 0)

    count = cells.shape[1]
    rows_at = lax.broadcasted_iota(jnp.int32, (ap, ap), 0)
    lanes_at = lax.broadcasted_iota(jnp.int32, (ap, ap), 1)
    flat = (cells[0:1, :] - slab * depth) * ap + cells[1:2, :]
    column = cells[2:3, :]
    hit = column == lax.broadcasted_iota(jnp.int32, (ap, count), 0)

    def place(row, values):
        vb[row : row + ap, :] = jnp.where(hit, values, 0.0).astype(jnp.bfloat16)

    for n in range(NT):
        rest = observed[n : n + 1, :]
        base = (n // 2) * 6 * ap + (n % 2) * ap
        for part in range(3):
            top = rest.astype(jnp.bfloat16).astype(f32)
            place(base + part * 2 * ap, top)
            rest = rest - top
    place(12 * ap, jnp.ones((1, count), f32))
    group = 4

    def spot(ch, carry):
        at = lax.broadcasted_iota(jnp.int32, (group * ap, count), 0) + ch * (group * ap)
        onehot = jnp.where(flat == at, 1.0, 0.0).astype(jnp.bfloat16)

        def times(row, width):
            return lax.dot_general(
                onehot, vb[row : row + width, :], (((1,), (1,)), ((), ())), preferred_element_type=f32
            )

        for pair in range(NT // 2):
            total = times(pair * 6 * ap, 2 * ap)
            total = total + times(pair * 6 * ap + 2 * ap, 2 * ap)
            total = total + times(pair * 6 * ap + 4 * ap, 2 * ap)
            total = total.reshape(group, ap, 2 * ap)
            ob[2 * pair, pl.ds(ch * group, group), :, :] = total[:, :, :ap]
            ob[2 * pair + 1, pl.ds(ch * group, group), :, :] = total[:, :, ap:]
        kc[pl.ds(ch * group, group), :, :] = times(12 * ap, ap).reshape(group, ap, ap)
        return carry

    lax.fori_loop(0, depth // group, spot, 0)

    def mark(d, carry):
        here = (rows_at == source[0, 1]) & (lanes_at == source[0, 2])
        deep = jnp.where(source[0, 0] == slab * depth + d, 1.0, 0.0)
        sf[d, :, :] = jnp.where(here, deep, 0.0)
        return carry

    lax.fori_loop(0, depth, mark, 0)

    my_rows = lax.broadcasted_iota(jnp.int32, (own, ap), 0) + lane_group * own
    my_lanes = lax.broadcasted_iota(jnp.int32, (own, ap), 1)
    home = pl.ds(pl.multiple_of(lane_group * own, own), own)

    def window_copy(i, o, spot_rows):
        return pltpu.make_async_remote_copy(
            src_ref=pack.at[i, o],
            dst_ref=win.at[i, :, spot_rows, :],
            send_sem=win_send.at[i, o],
            recv_sem=win_recv.at[i, o],
            device_id={"shot": half * 8 + peer(o), "slab": slab},
            device_id_type=MESH,
        )

    def rows_of(member):
        return pl.ds(pl.multiple_of(member * own, own), own)

    for i in range(2):
        loads[i].wait()
        swaps[i].wait_recv()

        def fill(d, carry):
            low = raw[0, i, d]
            high = raw[1, i, d]
            for o in range(8):
                member = half * 8 + (peer(o) if o < 7 else lane_group)
                keep_row = my_rows >= anchors[member, 0]
                keep_col = my_lanes >= anchors[member, 1]
                a = jnp.where(keep_col, low[:, :ap], low[:, ap:])
                b = jnp.where(keep_col, high[:, :ap], high[:, ap:])
                value = jnp.where(keep_row, a, b)
                if o < 7:
                    pack[i, o, d] = value
                else:
                    win[i, d, home, :] = value
            return carry

        lax.fori_loop(0, depth, fill, 0)
        for o in range(7):
            window_copy(i, o, home).start()

    row_anchor = anchors[shot, 0]
    col_anchor = anchors[shot, 1]

    def unwind(x, lane_shift, first_row):
        x = pltpu.roll(x, lane_shift, axis=1)
        tmp[:ap, :] = x
        tmp[ap:, :] = x
        return tmp[pl.ds(first_row, ap), :]

    back = (ap - col_anchor) % ap

    for o in range(7):
        window_copy(0, o, rows_of(origin(o))).wait_recv()

    def settle_buoyancy(d, carry):
        bz[d + 1, inner, :] = unwind(win[0, d], back, row_anchor)
        return carry

    lax.fori_loop(0, depth, settle_buoyancy, 0)
    go(halos[2 * NT])

    def sides(d, carry):
        for c0 in range(0, ap, CHUNK):
            rows = lax.broadcasted_iota(jnp.int32, (CHUNK, ap), 0) + c0
            lanes = lax.broadcasted_iota(jnp.int32, (CHUNK, ap), 1)
            x = bz[d + 1, PAD + c0 : PAD + c0 + CHUNK, :]
            prev = bz[d + 1, PAD + c0 - 1 : PAD + c0 - 1 + CHUNK, :]
            succ = bz[d + 1, PAD + c0 + 1 : PAD + c0 + 1 + CHUNK, :]
            face = 0.5 * (x + prev)
            total = face + 0.5 * (x + succ)
            cr[d, PAD + c0 : PAD + c0 + CHUNK, :] = jnp.where(rows == 0, 0.0, face)
            prev = jnp.where(lanes == 0, 0.0, pltpu.roll(x, 1, axis=1))
            succ = jnp.where(lanes == ap - 1, 0.0, pltpu.roll(x, ap - 1, axis=1))
            face = 0.5 * (x + prev)
            total = total + face + 0.5 * (x + succ)
            cc[d, c0 : c0 + CHUNK, :] = jnp.where(lanes == 0, 0.0, face)
            dg[d, c0 : c0 + CHUNK, :] = total
        return carry

    lax.fori_loop(0, depth, sides, 0)
    arrived(halos[2 * NT])

    def depths(d, carry):
        first = (slab == 0) & (d == 0)
        last = (slab == slabs - 1) & (d == depth - 1)
        for c0 in range(0, ap, CHUNK):
            span = slice(PAD + c0, PAD + c0 + CHUNK)
            x = bz[d + 1, span, :]
            prev = jnp.where(first, 0.0, bz[d, span, :])
            succ = jnp.where(last, 0.0, bz[d + 2, span, :])
            low = 0.5 * (x + prev)
            high = 0.5 * (x + succ)
            fd[d, c0 : c0 + CHUNK, :] = jnp.where(first, 0.0, low)
            fd[d + 1, c0 : c0 + CHUNK, :] = jnp.where(last, 0.0, high)
            dg[d, c0 : c0 + CHUNK, :] = dg[d, c0 : c0 + CHUNK, :] + low + high
        return carry

    lax.fori_loop(0, depth, depths, 0)

    def spread(field, d, c0):
        at = PAD + c0
        x = field[d + 1, at : at + CHUNK, :]
        across = cc[d, c0 : c0 + CHUNK, :]
        total = fd[d, c0 : c0 + CHUNK, :] * field[d, at : at + CHUNK, :]
        total = total + fd[d + 1, c0 : c0 + CHUNK, :] * field[d + 2, at : at + CHUNK, :]
        total = total + cr[d, at : at + CHUNK, :] * field[d + 1, at - 1 : at - 1 + CHUNK, :]
        total = total + cr[d, at + 1 : at + 1 + CHUNK, :] * field[d + 1, at + 1 : at + 1 + CHUNK, :]
        total = total + across * pltpu.roll(x, 1, axis=1)
        total = total + pltpu.roll(across * x, ap - 1, axis=1)
        return total - dg[d, c0 : c0 + CHUNK, :] * x, x

    def edges_first(step, after):
        lax.fori_loop(0, 2, lambda i, c: step(i * (depth - 1), c), 0)
        after()
        lax.fori_loop(1, depth - 1, step, 0)

    loads[2].wait()
    loads[3].wait()
    arrived(halos[0])

    def first_spread(d, carry):
        for c0 in range(0, ap, CHUNK):
            qb[0, d, c0 : c0 + CHUNK, :] = spread(pb.at[0], d, c0)[0]
        return carry

    lax.fori_loop(0, depth, first_spread, 0)

    for o in range(7):
        window_copy(1, o, rows_of(origin(o))).wait_recv()
    loads[4].wait()
    loads[5].wait()

    def first_step(d, carry):
        kp[d] = unwind(win[1, d], back, row_anchor)
        for c0 in range(0, ap, CHUNK):
            rows = slice(c0, c0 + CHUNK)
            at = slice(PAD + c0, PAD + c0 + CHUNK)
            k = kp[d, rows, :]
            nxt = 2.0 * pb[0, d + 1, at, :] - pm[d, rows, :] + k * qb[0, d, rows, :]
            pb[1, d + 1, at, :] = nxt + wavelet[0, 0] * sf[d, rows, :]
            wb[0, d + 1, at, :] = k * ab[1, d, rows, :]
        return carry

    def send_first():
        go(halos[1])
        go(halos[NT])

    edges_first(first_step, send_first)

    for n in range(1, NT):

        def forward(d, carry):
            for c0 in range(0, ap, CHUNK):
                rows = slice(c0, c0 + CHUNK)
                at = slice(PAD + c0, PAD + c0 + CHUNK)
                q, x = spread(pb.at[n], d, c0)
                qb[n, d, rows, :] = q
                nxt = 2.0 * x - pb[n - 1, d + 1, at, :] + kp[d, rows, :] * q
                pb[n + 1, d + 1, at, :] = nxt + wavelet[0, n] * sf[d, rows, :]
            return carry

        arrived(halos[n])
        edges_first(forward, (lambda: go(halos[n + 1])) if n + 1 < NT else (lambda: None))

    outs = [
        pltpu.make_async_copy(pb.at[NT - 1, body, inner, :], wave_out.at[0, 0], out_sem.at[0]),
        pltpu.make_async_copy(pb.at[NT, body, inner, :], wave_out.at[0, 1], out_sem.at[1]),
    ]
    outs[0].start()
    outs[1].start()

    for m in range(NT):
        n = NT - m

        def backward(d, carry):
            for c0 in range(0, ap, CHUNK):
                rows = slice(c0, c0 + CHUNK)
                at = slice(PAD + c0, PAD + c0 + CHUNK)
                q, _ = spread(wb.at[m], d, c0)
                now = 2.0 * ab[m + 1, d, rows, :] - ab[m, d, rows, :] + q
                now = now + (kc[d, rows, :] * pb[n, d + 1, at, :] - ob[n - 1, d, rows, :])
                ab[m + 2, d, rows, :] = now
                if n > 1:
                    wb[m + 1, d + 1, at, :] = kp[d, rows, :] * now
                term = now * qb[n - 1, d, rows, :]
                gb[d, rows, :] = term if m == 0 else gb[d, rows, :] + term
            return carry

        arrived(halos[NT + m])
        edges_first(backward, (lambda: go(halos[NT + m + 1])) if n > 1 else (lambda: None))

    outs += [
        pltpu.make_async_copy(ab.at[NT], adjoint_out.at[0, 0], out_sem.at[2]),
        pltpu.make_async_copy(ab.at[NT + 1], adjoint_out.at[0, 1], out_sem.at[3]),
    ]
    outs[2].start()
    outs[3].start()

    def wind(d, carry):
        gc[d] = unwind(gb[d], col_anchor % ap, ap - row_anchor)
        return carry

    lax.fori_loop(0, depth, wind, 0)

    def grad_copy(o, spot_rows):
        return pltpu.make_async_remote_copy(
            src_ref=gc.at[:, spot_rows, :],
            dst_ref=gr.at[o],
            send_sem=grad_send.at[o],
            recv_sem=grad_recv.at[o],
            device_id={"shot": half * 8 + peer(o), "slab": slab},
            device_id_type=MESH,
        )

    for o in range(7):
        grad_copy(o, rows_of(peer(o))).start()
    for o in range(7):
        grad_copy(o, rows_of(peer(o))).wait_recv()

    def collect(d, carry):
        parts = [jnp.zeros((own, ap), f32) for _ in range(4)]
        for o in range(8):
            value = gr[o, d] if o < 7 else gc[d, home, :]
            member = half * 8 + (origin(o) if o < 7 else lane_group)
            keep_row = my_rows >= anchors[member, 0]
            keep_col = my_lanes >= anchors[member, 1]
            low = jnp.where(keep_row, value, 0.0)
            high = jnp.where(keep_row, 0.0, value)
            parts[0] += jnp.where(keep_col, low, 0.0)
            parts[1] += jnp.where(keep_col, 0.0, low)
            parts[2] += jnp.where(keep_col, high, 0.0)
            parts[3] += jnp.where(keep_col, 0.0, high)
        acc[0, d, :, :ap] = parts[0]
        acc[0, d, :, ap:] = parts[1]
        acc[1, d, :, :ap] = parts[2]
        acc[1, d, :, ap:] = parts[3]
        return carry

    lax.fori_loop(0, depth, collect, 0)
    merge = pltpu.make_async_remote_copy(
        src_ref=acc.at[1 - half],
        dst_ref=pr,
        send_sem=swap_send.at[2],
        recv_sem=swap_recv.at[2],
        device_id={"shot": partner, "slab": slab},
        device_id_type=MESH,
    )
    merge.start()
    merge.wait_recv()

    def finish(d, carry):
        pr[d] = pr[d] + acc[half, d]
        return carry

    lax.fori_loop(0, depth, finish, 0)
    outs.append(pltpu.make_async_copy(pr, grad_out, out_sem.at[4]))
    outs[4].start()

    for swap in swaps:
        swap.wait_send()
    merge.wait_send()
    for pair in halos:
        pair[0].wait_send()
        pair[1].wait_send()
    for o in range(7):
        window_copy(0, o, home).wait_send()
        window_copy(1, o, home).wait_send()
        grad_copy(o, rows_of(peer(o))).wait_send()
    for copy in outs:
        copy.wait()


def shards(
    kappa,
    buoyancy,
    anchors,
    wave_start,
    adjoint_start,
    wavelet,
    source_cell,
    receiver_cells,
    observed,
):
    depth, own, side = kappa.shape
    ap = wave_start.shape[3]
    count = receiver_cells.shape[1]
    f32 = jnp.float32
    any_space = pl.BlockSpec(memory_space=pl.ANY)
    smem = pl.BlockSpec(memory_space=pltpu.SMEM)
    vmem = pl.BlockSpec(memory_space=pltpu.VMEM)
    padded = (depth + 2, ap + 2 * PAD, ap)
    plain = (depth, ap, ap)
    return pl.pallas_call(
        kernel,
        out_shape=(
            jax.ShapeDtypeStruct(kappa.shape, f32),
            jax.ShapeDtypeStruct(wave_start.shape, f32),
            jax.ShapeDtypeStruct(adjoint_start.shape, f32),
        ),
        in_specs=[smem, smem, smem, any_space, any_space, any_space, any_space, vmem, vmem],
        out_specs=(any_space, any_space, any_space),
        scratch_shapes=[
            pltpu.VMEM((2, 2, depth, own, side), f32),
            pltpu.VMEM((2, 7, depth, own, ap), f32),
            pltpu.VMEM((2,) + plain, f32),
            pltpu.VMEM((NT + 1,) + padded, f32),
            pltpu.VMEM(plain, f32),
            pltpu.VMEM((NT,) + plain, f32),
            pltpu.VMEM(plain, f32),
            pltpu.VMEM(padded, f32),
            pltpu.VMEM((depth + 1, ap, ap), f32),
            pltpu.VMEM((depth, ap + 2 * PAD, ap), f32),
            pltpu.VMEM(plain, f32),
            pltpu.VMEM(plain, f32),
            pltpu.VMEM((NT,) + padded, f32),
            pltpu.VMEM((NT + 2,) + plain, f32),
            pltpu.VMEM(plain, f32),
            pltpu.VMEM((NT,) + plain, f32),
            pltpu.VMEM(plain, f32),
            pltpu.VMEM((13 * ap, count), jnp.bfloat16),
            pltpu.VMEM(plain, f32),
            pltpu.VMEM(plain, f32),
            pltpu.VMEM((7, depth, own, ap), f32),
            pltpu.VMEM((2, depth, own, side), f32),
            pltpu.VMEM((depth, own, side), f32),
            pltpu.VMEM((2 * ap, ap), f32),
            pltpu.SemaphoreType.DMA((6,)),
            pltpu.SemaphoreType.DMA((3,)),
            pltpu.SemaphoreType.DMA((3,)),
            pltpu.SemaphoreType.DMA((2, 7)),
            pltpu.SemaphoreType.DMA((2, 7)),
            pltpu.SemaphoreType.DMA((2 * NT + 1, 2)),
            pltpu.SemaphoreType.DMA((2 * NT + 1, 2)),
            pltpu.SemaphoreType.DMA((7,)),
            pltpu.SemaphoreType.DMA((7,)),
            pltpu.SemaphoreType.DMA((5,)),
        ],
        compiler_params=pltpu.CompilerParams(
            collective_id=0, has_side_effects=True, vmem_limit_bytes=60 * 1024 * 1024
        ),
    )(
        anchors,
        wavelet,
        source_cell,
        kappa,
        buoyancy,
        wave_start,
        adjoint_start,
        receiver_cells[0].T,
        observed[0],
    )


def solution(mesh):
    in_specs = (
        P("slab", "shot", None),
        P("slab", "shot", None),
        P(),
        P("shot", None, "slab", None, None),
        P("shot", None, "slab", None, None),
        P("shot", None),
        P("shot", None),
        P("shot", None, None),
        P("shot", None, None),
    )
    out_specs = (
        P("slab", "shot", None),
        P("shot", None, "slab", None, None),
        P("shot", None, "slab", None, None),
    )
    return jax.shard_map(shards, mesh=mesh, in_specs=in_specs, out_specs=out_specs, check_vma=False)
```

```python
import jax
import jax.numpy as jnp
from jax import lax
from jax.experimental import pallas as pl
from jax.experimental.pallas import tpu as pltpu
from jax.sharding import PartitionSpec as P

MESH = pl.DeviceIdType.MESH
NT = 4
PAD = 8
CHUNK = 32
OFFSETS = ((2, 0), (2, 1), (1, 0), (3, 0), (1, 1), (3, 1), (0, 1))


def kernel(
    anchors,
    wavelet,
    source,
    kappa,
    buoyancy,
    wave,
    adjoint,
    cells,
    observed,
    grad_out,
    wave_out,
    adjoint_out,
    raw,
    pack,
    win,
    pb,
    qb,
    kp,
    bz,
    fd,
    cr,
    cc,
    dg,
    wb,
    ab,
    kc,
    ob,
    sf,
    vb,
    gb,
    gc,
    gr,
    acc,
    pr,
    tmp,
    load_sem,
    swap_send,
    swap_recv,
    win_send,
    win_recv,
    halo_send,
    halo_recv,
    grad_send,
    grad_recv,
    merge_send,
    merge_recv,
    out_sem,
):
    depth, own, side = kappa.shape
    ap = side // 2
    f32 = jnp.float32
    shot = lax.axis_index("shot")
    slab = lax.axis_index("slab")
    slabs = lax.axis_size("slab")
    half = shot // 8
    lane_group = shot % 8
    px = lane_group // 2
    pc = lane_group % 2
    partner = (shot + 8) % 16
    below = (slab + 1) % slabs
    above = (slab + slabs - 1) % slabs
    parts = depth // 4

    def peer(o):
        dx, dc = OFFSETS[o]
        return ((px + dx) % 4) * 2 + (pc + dc) % 2

    def origin(o):
        dx, dc = OFFSETS[o]
        return ((px + 4 - dx) % 4) * 2 + (pc + 2 - dc) % 2

    sent = []
    due = []

    def start_local(copy):
        copy.start()
        due.append((copy, copy.wait))

    def start_remote(copy):
        copy.start()
        sent.append(copy.wait_send)
        due.append((copy, copy.wait_recv))

    def finish_of(copy):
        for i, (known, wait) in enumerate(due):
            if known is copy or (isinstance(copy, tuple) and known == copy):
                due.pop(i)
                wait()
                return
        raise ValueError(copy)

    def remote(src, dst, send, recv, to_shot, to_slab):
        return pltpu.make_async_remote_copy(
            src_ref=src,
            dst_ref=dst,
            send_sem=send,
            recv_sem=recv,
            device_id={"shot": to_shot, "slab": to_slab},
            device_id_type=MESH,
        )

    inner = pl.ds(PAD, ap)
    body = pl.ds(1, depth)

    barrier = pltpu.get_barrier_semaphore()

    def greet(to_shot, to_slab):
        pl.semaphore_signal(
            barrier, inc=1, device_id={"shot": to_shot, "slab": to_slab}, device_id_type=MESH
        )

    greet(partner, slab)
    greet(shot, below)
    greet(shot, above)
    for o in range(7):
        greet(half * 8 + peer(o), slab)

    loads = [
        pltpu.make_async_copy(buoyancy, raw.at[half, 0], load_sem.at[0]),
        pltpu.make_async_copy(kappa, raw.at[half, 1], load_sem.at[1]),
        pltpu.make_async_copy(wave.at[0, 0], pb.at[0, body, inner, :], load_sem.at[2]),
        pltpu.make_async_copy(wave.at[0, 1], pb.at[1, body, inner, :], load_sem.at[3]),
        pltpu.make_async_copy(adjoint.at[0, 0], ab.at[0], load_sem.at[4]),
        pltpu.make_async_copy(adjoint.at[0, 1], ab.at[1], load_sem.at[5]),
    ]
    for copy in loads:
        start_local(copy)

    margin = jnp.zeros((PAD, ap), f32)

    def clear(i, carry):
        for n in range(NT):
            pb[n + 1, i + 1, :PAD, :] = margin
            pb[n + 1, i + 1, PAD + ap :, :] = margin
            wb[n, i + 1, :PAD, :] = margin
            wb[n, i + 1, PAD + ap :, :] = margin
        bz[i + 1, :PAD, :] = margin
        bz[i + 1, PAD + ap :, :] = margin
        cr[i, PAD + ap :, :] = margin
        return carry

    lax.fori_loop(0, depth, clear, 0)

    count = cells.shape[2]
    rows_at = lax.broadcasted_iota(jnp.int32, (ap, ap), 0)
    lanes_at = lax.broadcasted_iota(jnp.int32, (ap, ap), 1)
    flat = (cells[0] - slab * depth) * ap + cells[1]
    hit = cells[2] == lax.broadcasted_iota(jnp.int32, (ap, count), 0)

    def place(row, values):
        vb[row : row + ap, :] = jnp.where(hit, values, 0.0).astype(jnp.bfloat16)

    for n in range(NT):
        rest = observed[n : n + 1, :]
        base = (n // 2) * 6 * ap + (n % 2) * ap
        for part in range(3):
            top = rest.astype(jnp.bfloat16).astype(f32)
            place(base + part * 2 * ap, top)
            rest = rest - top
    place(12 * ap, jnp.ones((1, count), f32))

    def mark(d, carry):
        here = (rows_at == source[0, 1]) & (lanes_at == source[0, 2])
        deep = jnp.where(source[0, 0] == slab * depth + d, 1.0, 0.0)
        sf[d, :, :] = jnp.where(here, deep, 0.0)
        return carry

    lax.fori_loop(0, depth, mark, 0)

    group = depth // parts

    def spot(ch):
        at = lax.broadcasted_iota(jnp.int32, (group * ap, count), 0) + ch * (group * ap)
        onehot = jnp.where(flat == at, 1.0, 0.0).astype(jnp.bfloat16)

        def times(row, width):
            return lax.dot_general(
                onehot, vb[row : row + width, :], (((1,), (1,)), ((), ())), preferred_element_type=f32
            )

        for pair in range(NT // 2):
            total = times(pair * 6 * ap, 2 * ap)
            total = total + times(pair * 6 * ap + 2 * ap, 2 * ap)
            total = total + times(pair * 6 * ap + 4 * ap, 2 * ap)
            total = total.reshape(group, ap, 2 * ap)
            ob[2 * pair, pl.ds(ch * group, group), :, :] = total[:, :, :ap]
            ob[2 * pair + 1, pl.ds(ch * group, group), :, :] = total[:, :, ap:]
        kc[pl.ds(ch * group, group), :, :] = times(12 * ap, ap).reshape(group, ap, ap)

    pl.semaphore_wait(barrier, 10)

    def plane_of(q, p):
        return 2 * q + p + (p // 2) * (depth - 4 - 4 * q)

    swaps = []
    for q in range(parts):
        swaps.append([])
        for i, ref in enumerate((buoyancy, kappa)):
            for e in range(2):
                planes = pl.ds(plane_of(q, 2 * e), 2)
                swaps[q].append(
                    remote(
                        ref.at[planes],
                        raw.at[half, i, planes],
                        swap_send.at[q, i, e],
                        swap_recv.at[q, i, e],
                        partner,
                        slab,
                    )
                )

    def swap_part(q):
        for copy in swaps[q]:
            start_remote(copy)

    def field_halo(slot, field, src=None):
        first = field.at[1, inner, :] if src is None else src.at[0]
        last = field.at[depth, inner, :] if src is None else src.at[depth - 1]
        return (
            remote(
                first,
                field.at[depth + 1, inner, :],
                halo_send.at[slot, 0],
                halo_recv.at[slot, 0],
                shot,
                above,
            ),
            remote(
                last,
                field.at[0, inner, :],
                halo_send.at[slot, 1],
                halo_recv.at[slot, 1],
                shot,
                below,
            ),
        )

    wave_halo = [field_halo(0, pb.at[1], wave.at[0, 1])]
    wave_halo += [field_halo(n, pb.at[n + 1]) for n in range(1, NT)]
    back_halo = [field_halo(NT + m, wb.at[m]) for m in range(NT)]
    buoy_halo = field_halo(2 * NT, bz)

    def go(pair):
        start_remote(pair[0])
        start_remote(pair[1])

    def arrived(pair):
        finish_of(pair[0])
        finish_of(pair[1])

    swap_part(0)
    swap_part(1)

    my_rows = lax.broadcasted_iota(jnp.int32, (own, ap), 0) + lane_group * own
    my_lanes = lax.broadcasted_iota(jnp.int32, (own, ap), 1)

    def rows_of(member):
        return pl.ds(pl.multiple_of(member * own, own), own)

    home = rows_of(lane_group)

    def window_copy(q, o, spot_rows):
        return remote(
            pack.at[q, o],
            win.at[q, :, :, spot_rows, :],
            win_send.at[q, o],
            win_recv.at[q, o],
            half * 8 + peer(o),
            slab,
        )

    finish_of(loads[0])
    finish_of(loads[1])
    for q in range(parts):
        for copy in swaps[q]:
            finish_of(copy)

        def fill(p, carry):
            d = plane_of(q, p)
            for i in range(2):
                low = raw[0, i, d]
                high = raw[1, i, d]
                for o in range(8):
                    member = half * 8 + (peer(o) if o < 7 else lane_group)
                    keep_row = my_rows >= anchors[0, member]
                    keep_col = my_lanes >= anchors[1, member]
                    a = jnp.where(keep_col, low[:, :ap], low[:, ap:])
                    b = jnp.where(keep_col, high[:, :ap], high[:, ap:])
                    value = jnp.where(keep_row, a, b)
                    if o < 7:
                        pack[q, o, i, p] = value
                    else:
                        win[q, i, p, home, :] = value
            return carry

        lax.fori_loop(0, 4, fill, 0)
        for o in range(7):
            copy = window_copy(q, o, home)
            copy.start()
            sent.append(copy.wait_send)
            landing = window_copy(q, o, rows_of(origin(o)))
            due.append(((q, o), landing.wait_recv))
        if q + 2 < parts:
            swap_part(q + 2)
        elif q + 2 == parts:
            go(wave_halo[0])
        spot(q)

    row_anchor = anchors[0, shot]
    col_anchor = anchors[1, shot]

    def unwind(x, lane_shift, first_row):
        x = pltpu.roll(x, lane_shift, axis=1)
        tmp[:ap, :] = x
        tmp[ap:, :] = x
        return tmp[pl.ds(first_row, ap), :]

    lane_back = (ap - col_anchor) % ap

    def settle(q):
        for o in range(7):
            finish_of((q, o))

        def one(p, carry):
            d = plane_of(q, p)
            bz[d + 1, inner, :] = unwind(win[q, 0, p], lane_back, row_anchor)
            k = unwind(win[q, 1, p], lane_back, row_anchor)
            kp[d] = k
            wb[0, d + 1, inner, :] = k * ab[1, d]
            return carry

        lax.fori_loop(0, 4, one, 0)

    def each(low, high, step):
        def both(i, carry):
            d = low + i // 2
            step(d + (i % 2) * (depth - 1 - 2 * d))
            return carry

        lax.fori_loop(0, 2 * (high - low), both, 0)

    def coefficients(d):
        first = (slab == 0) & (d == 0)
        last = (slab == slabs - 1) & (d == depth - 1)
        for c0 in range(0, ap, CHUNK):
            rows = lax.broadcasted_iota(jnp.int32, (CHUNK, ap), 0) + c0
            lanes = lax.broadcasted_iota(jnp.int32, (CHUNK, ap), 1)
            at = slice(PAD + c0, PAD + c0 + CHUNK)
            x = bz[d + 1, at, :]
            prev = bz[d + 1, PAD + c0 - 1 : PAD + c0 - 1 + CHUNK, :]
            succ = bz[d + 1, PAD + c0 + 1 : PAD + c0 + 1 + CHUNK, :]
            face = 0.5 * (x + prev)
            total = face + 0.5 * (x + succ)
            cr[d, at, :] = jnp.where(rows == 0, 0.0, face)
            prev = jnp.where(lanes == 0, 0.0, pltpu.roll(x, 1, axis=1))
            succ = jnp.where(lanes == ap - 1, 0.0, pltpu.roll(x, ap - 1, axis=1))
            face = 0.5 * (x + prev)
            total = total + face + 0.5 * (x + succ)
            cc[d, c0 : c0 + CHUNK, :] = jnp.where(lanes == 0, 0.0, face)
            low = 0.5 * (x + jnp.where(first, 0.0, bz[d, at, :]))
            high = 0.5 * (x + jnp.where(last, 0.0, bz[d + 2, at, :]))
            fd[d, c0 : c0 + CHUNK, :] = jnp.where(first, 0.0, low)
            fd[d + 1, c0 : c0 + CHUNK, :] = jnp.where(last, 0.0, high)
            dg[d, c0 : c0 + CHUNK, :] = total + low + high

    def spread(field, d, c0):
        at = PAD + c0
        x = field[d + 1, at : at + CHUNK, :]
        across = cc[d, c0 : c0 + CHUNK, :]
        total = fd[d, c0 : c0 + CHUNK, :] * field[d, at : at + CHUNK, :]
        total = total + fd[d + 1, c0 : c0 + CHUNK, :] * field[d + 2, at : at + CHUNK, :]
        total = total + cr[d, at : at + CHUNK, :] * field[d + 1, at - 1 : at - 1 + CHUNK, :]
        total = total + cr[d, at + 1 : at + 1 + CHUNK, :] * field[d + 1, at + 1 : at + 1 + CHUNK, :]
        total = total + across * pltpu.roll(x, 1, axis=1)
        total = total + pltpu.roll(across * x, ap - 1, axis=1)
        return total - dg[d, c0 : c0 + CHUNK, :] * x, x

    def forward(n):
        def step(d):
            for c0 in range(0, ap, CHUNK):
                rows = slice(c0, c0 + CHUNK)
                at = slice(PAD + c0, PAD + c0 + CHUNK)
                q, x = spread(pb.at[n + 1], d, c0)
                qb[n, d, rows, :] = q
                nxt = 2.0 * x - pb[n, d + 1, at, :] + kp[d, rows, :] * q
                pb[n + 2, d + 1, at, :] = nxt + wavelet[0, n] * sf[d, rows, :]

        return step

    def backward(n):
        m = NT - n

        def step(d):
            for c0 in range(0, ap, CHUNK):
                rows = slice(c0, c0 + CHUNK)
                at = slice(PAD + c0, PAD + c0 + CHUNK)
                q, _ = spread(wb.at[m], d, c0)
                now = 2.0 * ab[m + 1, d, rows, :] - ab[m, d, rows, :] + q
                now = now + (kc[d, rows, :] * pb[n + 1, d + 1, at, :] - ob[n - 1, d, rows, :])
                ab[m + 2, d, rows, :] = now
                if n > 1:
                    wb[m + 1, d + 1, at, :] = kp[d, rows, :] * now
                term = now * qb[n - 1, d, rows, :]
                gb[d, rows, :] = term if m == 0 else gb[d, rows, :] + term

        return step

    groups = ((4, 8, 0), (2, 4, 8), (0, 2, 12))

    def slot_of(r, d):
        low, high, base = groups[r]
        upper = d // (depth // 2)
        return base + d - low - upper * (depth - 2 * high)

    def grad_copy(r, o, spot_rows):
        low, high, base = groups[r]
        places = pl.ds(base, 2 * (high - low))
        return remote(
            gc.at[places, spot_rows, :],
            gr.at[o, places],
            grad_send.at[r, o],
            grad_recv.at[r, o],
            half * 8 + peer(o),
            slab,
        )

    pieces = [[grad_copy(r, o, rows_of(peer(o))) for o in range(7)] for r in range(3)]
    merges = []
    for r, (low, high, base) in enumerate(groups):
        places = pl.ds(base, 2 * (high - low))
        merges.append(
            remote(
                acc.at[1 - half, places],
                pr.at[places],
                merge_send.at[r],
                merge_recv.at[r],
                partner,
                slab,
            )
        )

    def hand_in(r):
        low, high, _ = groups[r]

        def wind(d):
            gc[slot_of(r, d)] = unwind(gb[d], col_anchor % ap, ap - row_anchor)

        each(low, high, wind)
        for copy in pieces[r]:
            start_remote(copy)

    def collect(r):
        low, high, base = groups[r]
        for copy in pieces[r]:
            finish_of(copy)

        def one(t, carry):
            sums = [jnp.zeros((own, ap), f32) for _ in range(4)]
            for o in range(8):
                value = gr[o, t] if o < 7 else gc[t, home, :]
                member = half * 8 + (origin(o) if o < 7 else lane_group)
                keep_row = my_rows >= anchors[0, member]
                keep_col = my_lanes >= anchors[1, member]
                top = jnp.where(keep_row, value, 0.0)
                bottom = jnp.where(keep_row, 0.0, value)
                sums[0] += jnp.where(keep_col, top, 0.0)
                sums[1] += jnp.where(keep_col, 0.0, top)
                sums[2] += jnp.where(keep_col, bottom, 0.0)
                sums[3] += jnp.where(keep_col, 0.0, bottom)
            acc[0, t, :, :ap] = sums[0]
            acc[0, t, :, ap:] = sums[1]
            acc[1, t, :, :ap] = sums[2]
            acc[1, t, :, ap:] = sums[3]
            return carry

        lax.fori_loop(base, base + 2 * (high - low), one, 0)
        start_remote(merges[r])

    def finish(r):
        low, high, base = groups[r]
        finish_of(merges[r])

        def one(t, carry):
            pr[t] = pr[t] + acc[half, t]
            return carry

        lax.fori_loop(base, base + 2 * (high - low), one, 0)
        size = high - low
        for e in range(2):
            start_local(
                pltpu.make_async_copy(
                    pr.at[pl.ds(base + e * size, size)],
                    grad_out.at[pl.ds(low if e == 0 else depth - high, size)],
                    out_sem.at[4 + 2 * r + e],
                )
            )

    for i in range(2, 6):
        finish_of(loads[i])
    settle(0)
    go(buoy_halo)
    settle(1)
    arrived(buoy_halo)
    arrived(wave_halo[0])
    coefficients_first = 3
    each(0, coefficients_first, coefficients)
    each(0, 1, forward(0))
    go(wave_halo[1])
    each(1, 3, forward(0))
    go(back_halo[0])
    settle(2)
    each(3, 5, coefficients)
    each(3, 5, forward(0))
    arrived(wave_halo[1])
    each(0, 1, forward(1))
    go(wave_halo[2])
    each(1, 4, forward(1))
    settle(3)
    each(5, 8, coefficients)
    each(5, 8, forward(0))
    arrived(wave_halo[2])
    each(0, 1, forward(2))
    go(wave_halo[3])
    each(4, 8, forward(1))
    each(1, 8, forward(2))
    arrived(back_halo[0])
    arrived(wave_halo[3])
    each(0, 1, forward(3))
    each(0, 1, backward(4))
    go(back_halo[1])
    each(1, 8, forward(3))
    start_local(pltpu.make_async_copy(pb.at[NT, body, inner, :], wave_out.at[0, 0], out_sem.at[0]))
    start_local(pltpu.make_async_copy(pb.at[NT + 1, body, inner, :], wave_out.at[0, 1], out_sem.at[1]))
    each(1, 8, backward(4))
    each(2, 8, backward(3))
    each(3, 8, backward(2))
    each(4, 8, backward(1))
    hand_in(0)
    arrived(back_halo[1])
    each(0, 1, backward(3))
    go(back_halo[2])
    each(1, 2, backward(3))
    each(1, 3, backward(2))
    each(2, 4, backward(1))
    hand_in(1)
    arrived(back_halo[2])
    each(0, 1, backward(2))
    go(back_halo[3])
    start_local(pltpu.make_async_copy(ab.at[NT], adjoint_out.at[0, 0], out_sem.at[2]))
    each(1, 2, backward(1))
    collect(0)
    arrived(back_halo[3])
    each(0, 1, backward(1))
    hand_in(2)
    start_local(pltpu.make_async_copy(ab.at[NT + 1], adjoint_out.at[0, 1], out_sem.at[3]))
    collect(1)
    finish(0)
    collect(2)
    finish(1)
    finish(2)
    for wait in sent:
        wait()
    for _, wait in due:
        wait()


def shards(
    kappa,
    buoyancy,
    anchors,
    wave_start,
    adjoint_start,
    wavelet,
    source_cell,
    receiver_cells,
    observed,
):
    depth, own, side = kappa.shape
    ap = wave_start.shape[3]
    count = receiver_cells.shape[1]
    parts = depth // 4
    f32 = jnp.float32
    any_space = pl.BlockSpec(memory_space=pl.ANY)
    smem = pl.BlockSpec(memory_space=pltpu.SMEM)
    vmem = pl.BlockSpec(memory_space=pltpu.VMEM)
    padded = (depth + 2, ap + 2 * PAD, ap)
    plain = (depth, ap, ap)
    return pl.pallas_call(
        kernel,
        out_shape=(
            jax.ShapeDtypeStruct(kappa.shape, f32),
            jax.ShapeDtypeStruct(wave_start.shape, f32),
            jax.ShapeDtypeStruct(adjoint_start.shape, f32),
        ),
        in_specs=[smem, smem, smem, any_space, any_space, any_space, any_space, vmem, vmem],
        out_specs=(any_space, any_space, any_space),
        scratch_shapes=[
            pltpu.VMEM((2, 2, depth, own, side), f32),
            pltpu.VMEM((parts, 7, 2, 4, own, ap), f32),
            pltpu.VMEM((parts, 2, 4, ap, ap), f32),
            pltpu.VMEM((NT + 2,) + padded, f32),
            pltpu.VMEM((NT,) + plain, f32),
            pltpu.VMEM(plain, f32),
            pltpu.VMEM(padded, f32),
            pltpu.VMEM((depth + 1, ap, ap), f32),
            pltpu.VMEM((depth, ap + 2 * PAD, ap), f32),
            pltpu.VMEM(plain, f32),
            pltpu.VMEM(plain, f32),
            pltpu.VMEM((NT,) + padded, f32),
            pltpu.VMEM((NT + 2,) + plain, f32),
            pltpu.VMEM(plain, f32),
            pltpu.VMEM((NT,) + plain, f32),
            pltpu.VMEM(plain, f32),
            pltpu.VMEM((13 * ap, count), jnp.bfloat16),
            pltpu.VMEM(plain, f32),
            pltpu.VMEM(plain, f32),
            pltpu.VMEM((7, depth, own, ap), f32),
            pltpu.VMEM((2, depth, own, side), f32),
            pltpu.VMEM((depth, own, side), f32),
            pltpu.VMEM((2 * ap, ap), f32),
            pltpu.SemaphoreType.DMA((6,)),
            pltpu.SemaphoreType.DMA((parts, 2, 2)),
            pltpu.SemaphoreType.DMA((parts, 2, 2)),
            pltpu.SemaphoreType.DMA((parts, 7)),
            pltpu.SemaphoreType.DMA((parts, 7)),
            pltpu.SemaphoreType.DMA((2 * NT + 1, 2)),
            pltpu.SemaphoreType.DMA((2 * NT + 1, 2)),
            pltpu.SemaphoreType.DMA((3, 7)),
            pltpu.SemaphoreType.DMA((3, 7)),
            pltpu.SemaphoreType.DMA((3,)),
            pltpu.SemaphoreType.DMA((3,)),
            pltpu.SemaphoreType.DMA((10,)),
        ],
        compiler_params=pltpu.CompilerParams(
            collective_id=0, has_side_effects=True, vmem_limit_bytes=60 * 1024 * 1024
        ),
    )(
        anchors.T,
        wavelet,
        source_cell,
        kappa,
        buoyancy,
        wave_start,
        adjoint_start,
        jnp.transpose(receiver_cells, (2, 0, 1)),
        observed[0],
    )


def solution(mesh):
    in_specs = (
        P("slab", "shot", None),
        P("slab", "shot", None),
        P(),
        P("shot", None, "slab", None, None),
        P("shot", None, "slab", None, None),
        P("shot", None),
        P("shot", None),
        P("shot", None, None),
        P("shot", None, None),
    )
    out_specs = (
        P("slab", "shot", None),
        P("shot", None, "slab", None, None),
        P("shot", None, "slab", None, None),
    )
    return jax.shard_map(shards, mesh=mesh, in_specs=in_specs, out_specs=out_specs, check_vma=False)
```

```python
import jax
import jax.numpy as jnp
from jax import lax
from jax.experimental import pallas as pl
from jax.experimental.pallas import tpu as pltpu
from jax.sharding import PartitionSpec as P

MESH = pl.DeviceIdType.MESH
NT = 4
PAD = 8
CHUNK = 32
PARTS = ((0, 1), (1, 3), (3, 5), (5, 8))
RETURNS = ((4, 8), (2, 4), (1, 2), (0, 1))
OFFSETS = ((2, 0), (2, 1), (1, 0), (3, 0), (1, 1), (3, 1), (0, 1))


def kernel(
    anchors,
    wavelet,
    source,
    kappa,
    buoyancy,
    wave,
    adjoint,
    cells,
    observed,
    grad_out,
    wave_out,
    adjoint_out,
    raw,
    pack,
    win,
    pb,
    qb,
    kp,
    bz,
    fd,
    cr,
    cc,
    dg,
    wb,
    ab,
    kc,
    ob,
    sf,
    vb,
    gb,
    gc,
    gr,
    acc,
    pr,
    tmp,
    load_sem,
    swap_send,
    swap_recv,
    win_send,
    win_recv,
    halo_send,
    halo_recv,
    grad_send,
    grad_recv,
    merge_send,
    merge_recv,
    out_sem,
):
    depth, own, side = kappa.shape
    ap = side // 2
    f32 = jnp.float32
    shot = lax.axis_index("shot")
    slab = lax.axis_index("slab")
    slabs = lax.axis_size("slab")
    half = shot // 8
    lane_group = shot % 8
    px = lane_group // 2
    pc = lane_group % 2
    partner = (shot + 8) % 16
    below = (slab + 1) % slabs
    above = (slab + slabs - 1) % slabs

    def peer(o):
        dx, dc = OFFSETS[o]
        return ((px + dx) % 4) * 2 + (pc + dc) % 2

    def origin(o):
        dx, dc = OFFSETS[o]
        return ((px + 4 - dx) % 4) * 2 + (pc + 2 - dc) % 2

    sent = []
    due = []

    def start_local(copy):
        copy.start()
        due.append((copy, copy.wait))

    def start_remote(copy):
        copy.start()
        sent.append(copy.wait_send)
        due.append((copy, copy.wait_recv))

    def finish_of(copy):
        for i, (known, wait) in enumerate(due):
            if known is copy or (isinstance(copy, tuple) and known == copy):
                due.pop(i)
                wait()
                return
        raise ValueError(copy)

    def remote(src, dst, send, recv, to_shot, to_slab):
        return pltpu.make_async_remote_copy(
            src_ref=src,
            dst_ref=dst,
            send_sem=send,
            recv_sem=recv,
            device_id={"shot": to_shot, "slab": to_slab},
            device_id_type=MESH,
        )

    inner = pl.ds(PAD, ap)
    body = pl.ds(1, depth)

    barrier = pltpu.get_barrier_semaphore()

    def greet(to_shot, to_slab):
        pl.semaphore_signal(
            barrier, inc=1, device_id={"shot": to_shot, "slab": to_slab}, device_id_type=MESH
        )

    greet(partner, slab)
    greet(shot, below)
    greet(shot, above)
    for o in range(7):
        greet(half * 8 + peer(o), slab)

    loads = [
        pltpu.make_async_copy(buoyancy, raw.at[half, 0], load_sem.at[0]),
        pltpu.make_async_copy(kappa, raw.at[half, 1], load_sem.at[1]),
        pltpu.make_async_copy(wave.at[0, 0], pb.at[0, body, inner, :], load_sem.at[2]),
        pltpu.make_async_copy(wave.at[0, 1], pb.at[1, body, inner, :], load_sem.at[3]),
        pltpu.make_async_copy(adjoint.at[0, 0], ab.at[0], load_sem.at[4]),
        pltpu.make_async_copy(adjoint.at[0, 1], ab.at[1], load_sem.at[5]),
    ]
    for copy in loads:
        start_local(copy)

    margin = jnp.zeros((PAD, ap), f32)

    def clear(i, carry):
        for n in range(NT):
            pb[n + 1, i + 1, :PAD, :] = margin
            pb[n + 1, i + 1, PAD + ap :, :] = margin
            wb[n, i + 1, :PAD, :] = margin
            wb[n, i + 1, PAD + ap :, :] = margin
        bz[i + 1, :PAD, :] = margin
        bz[i + 1, PAD + ap :, :] = margin
        cr[i, PAD + ap :, :] = margin
        return carry

    lax.fori_loop(0, depth, clear, 0)

    count = cells.shape[2]
    rows_at = lax.broadcasted_iota(jnp.int32, (ap, ap), 0)
    lanes_at = lax.broadcasted_iota(jnp.int32, (ap, ap), 1)
    flat = (cells[0] - slab * depth) * ap + cells[1]
    hit = cells[2] == lax.broadcasted_iota(jnp.int32, (ap, count), 0)

    def place(row, values):
        vb[row : row + ap, :] = jnp.where(hit, values, 0.0).astype(jnp.bfloat16)

    for n in range(NT):
        rest = observed[n : n + 1, :]
        base = (n // 2) * 6 * ap + (n % 2) * ap
        for part in range(3):
            top = rest.astype(jnp.bfloat16).astype(f32)
            place(base + part * 2 * ap, top)
            rest = rest - top
    place(12 * ap, jnp.ones((1, count), f32))

    def mark(d, carry):
        here = (rows_at == source[0, 1]) & (lanes_at == source[0, 2])
        deep = jnp.where(source[0, 0] == slab * depth + d, 1.0, 0.0)
        sf[d, :, :] = jnp.where(here, deep, 0.0)
        return carry

    lax.fori_loop(0, depth, mark, 0)

    group = 4

    def spot(ch):
        at = lax.broadcasted_iota(jnp.int32, (group * ap, count), 0) + ch * (group * ap)
        onehot = jnp.where(flat == at, 1.0, 0.0).astype(jnp.bfloat16)

        def times(row, width):
            return lax.dot_general(
                onehot, vb[row : row + width, :], (((1,), (1,)), ((), ())), preferred_element_type=f32
            )

        for pair in range(NT // 2):
            total = times(pair * 6 * ap, 2 * ap)
            total = total + times(pair * 6 * ap + 2 * ap, 2 * ap)
            total = total + times(pair * 6 * ap + 4 * ap, 2 * ap)
            total = total.reshape(group, ap, 2 * ap)
            ob[2 * pair, pl.ds(ch * group, group), :, :] = total[:, :, :ap]
            ob[2 * pair + 1, pl.ds(ch * group, group), :, :] = total[:, :, ap:]
        kc[pl.ds(ch * group, group), :, :] = times(12 * ap, ap).reshape(group, ap, ap)

    pl.semaphore_wait(barrier, 10)

    def plane_of(span, p):
        low, high = span
        width = high - low
        return low + p + (p // width) * (depth - high - low - width)

    def places_of(span):
        low, high = span
        return pl.ds(2 * low, 2 * (high - low))

    swaps = []
    for q, (low, high) in enumerate(PARTS):
        swaps.append([])
        for i, ref in enumerate((buoyancy, kappa)):
            for e in range(2):
                planes = pl.ds(low if e == 0 else depth - high, high - low)
                swaps[q].append(
                    remote(
                        ref.at[planes],
                        raw.at[half, i, planes],
                        swap_send.at[q, i, e],
                        swap_recv.at[q, i, e],
                        partner,
                        slab,
                    )
                )

    def swap_part(q):
        for copy in swaps[q]:
            start_remote(copy)

    def field_halo(slot, field, src=None):
        first = field.at[1, inner, :] if src is None else src.at[0]
        last = field.at[depth, inner, :] if src is None else src.at[depth - 1]
        return (
            remote(
                first,
                field.at[depth + 1, inner, :],
                halo_send.at[slot, 0],
                halo_recv.at[slot, 0],
                shot,
                above,
            ),
            remote(
                last,
                field.at[0, inner, :],
                halo_send.at[slot, 1],
                halo_recv.at[slot, 1],
                shot,
                below,
            ),
        )

    wave_halo = [field_halo(0, pb.at[1], wave.at[0, 1])]
    wave_halo += [field_halo(n, pb.at[n + 1]) for n in range(1, NT)]
    back_halo = [field_halo(NT + m, wb.at[m]) for m in range(NT)]
    buoy_halo = field_halo(2 * NT, bz)

    def go(pair):
        start_remote(pair[0])
        start_remote(pair[1])

    def arrived(pair):
        finish_of(pair[0])
        finish_of(pair[1])

    swap_part(0)
    swap_part(1)

    my_rows = lax.broadcasted_iota(jnp.int32, (own, ap), 0) + lane_group * own
    my_lanes = lax.broadcasted_iota(jnp.int32, (own, ap), 1)

    def rows_of(member):
        return pl.ds(pl.multiple_of(member * own, own), own)

    home = rows_of(lane_group)

    def window_copy(q, o, spot_rows):
        return remote(
            pack.at[o, places_of(PARTS[q])],
            win.at[places_of(PARTS[q]), :, spot_rows, :],
            win_send.at[q, o],
            win_recv.at[q, o],
            half * 8 + peer(o),
            slab,
        )

    finish_of(loads[0])
    finish_of(loads[1])
    for q, part in enumerate(PARTS):
        for copy in swaps[q]:
            finish_of(copy)

        def fill(p, carry):
            d = plane_of(part, p)
            t = 2 * part[0] + p
            for i in range(2):
                low = raw[0, i, d]
                high = raw[1, i, d]
                for o in range(8):
                    member = half * 8 + (peer(o) if o < 7 else lane_group)
                    keep_row = my_rows >= anchors[0, member]
                    keep_col = my_lanes >= anchors[1, member]
                    a = jnp.where(keep_col, low[:, :ap], low[:, ap:])
                    b = jnp.where(keep_col, high[:, :ap], high[:, ap:])
                    value = jnp.where(keep_row, a, b)
                    if o < 7:
                        pack[o, t, i] = value
                    else:
                        win[t, i, home, :] = value
            return carry

        lax.fori_loop(0, 2 * (part[1] - part[0]), fill, 0)
        for o in range(7):
            copy = window_copy(q, o, home)
            copy.start()
            sent.append(copy.wait_send)
            landing = window_copy(q, o, rows_of(origin(o)))
            due.append(((q, o), landing.wait_recv))
        if q + 2 < len(PARTS):
            swap_part(q + 2)
        elif q + 2 == len(PARTS):
            go(wave_halo[0])
        spot(q)

    row_anchor = anchors[0, shot]
    col_anchor = anchors[1, shot]

    def unwind(values, lane_shift, first_row):
        for t, x in enumerate(values):
            x = pltpu.roll(x, lane_shift, axis=1)
            tmp[t, :ap, :] = x
            tmp[t, ap:, :] = x
        return [tmp[t, pl.ds(first_row, ap), :] for t in range(len(values))]

    lane_back = (ap - col_anchor) % ap

    def settle(q):
        low, high = PARTS[q]
        width = high - low
        for o in range(7):
            finish_of((q, o))

        def one(p, carry):
            t = 2 * low + p
            values = [win[t, 0], win[t, 1], win[t + width, 0], win[t + width, 1]]
            values = unwind(values, lane_back, row_anchor)
            products = []
            for e in range(2):
                d = low + p if e == 0 else depth - high + p
                products.append(values[2 * e + 1] * ab[1, d])
            for e in range(2):
                d = low + p if e == 0 else depth - high + p
                bz[d + 1, inner, :] = values[2 * e]
                kp[d] = values[2 * e + 1]
                wb[0, d + 1, inner, :] = products[e]
            return carry

        lax.fori_loop(0, width, one, 0)

    def each(low, high, step):
        pairs = 2 if (high - low) % 2 == 0 else 1

        def some(i, carry):
            layers = []
            for t in range(pairs):
                d = low + i * pairs + t
                layers += [d, depth - 1 - d]
            for c0 in range(0, ap, CHUNK):
                stores = [step(d, c0) for d in layers]
                for store in stores:
                    store()
            return carry

        lax.fori_loop(0, (high - low) // pairs, some, 0)

    def coefficients(d, c0):
        first = (slab == 0) & (d == 0)
        last = (slab == slabs - 1) & (d == depth - 1)
        rows = lax.broadcasted_iota(jnp.int32, (CHUNK, ap), 0) + c0
        lanes = lax.broadcasted_iota(jnp.int32, (CHUNK, ap), 1)
        at = slice(PAD + c0, PAD + c0 + CHUNK)
        x = bz[d + 1, at, :]
        prev = bz[d + 1, PAD + c0 - 1 : PAD + c0 - 1 + CHUNK, :]
        succ = bz[d + 1, PAD + c0 + 1 : PAD + c0 + 1 + CHUNK, :]
        across = 0.5 * (x + prev)
        total = across + 0.5 * (x + succ)
        across = jnp.where(rows == 0, 0.0, across)
        prev = jnp.where(lanes == 0, 0.0, pltpu.roll(x, 1, axis=1))
        succ = jnp.where(lanes == ap - 1, 0.0, pltpu.roll(x, ap - 1, axis=1))
        along = 0.5 * (x + prev)
        total = total + along + 0.5 * (x + succ)
        along = jnp.where(lanes == 0, 0.0, along)
        low = 0.5 * (x + jnp.where(first, 0.0, bz[d, at, :]))
        high = 0.5 * (x + jnp.where(last, 0.0, bz[d + 2, at, :]))
        total = total + low + high
        low = jnp.where(first, 0.0, low)
        high = jnp.where(last, 0.0, high)

        def store():
            cr[d, at, :] = across
            cc[d, c0 : c0 + CHUNK, :] = along
            fd[d, c0 : c0 + CHUNK, :] = low
            fd[d + 1, c0 : c0 + CHUNK, :] = high
            dg[d, c0 : c0 + CHUNK, :] = total

        return store

    def spread(field, d, c0):
        at = PAD + c0
        x = field[d + 1, at : at + CHUNK, :]
        across = cc[d, c0 : c0 + CHUNK, :]
        sides = across * pltpu.roll(x, 1, axis=1)
        sides = sides + pltpu.roll(across * x, ap - 1, axis=1)
        total = fd[d, c0 : c0 + CHUNK, :] * field[d, at : at + CHUNK, :]
        total = total + fd[d + 1, c0 : c0 + CHUNK, :] * field[d + 2, at : at + CHUNK, :]
        total = total + cr[d, at : at + CHUNK, :] * field[d + 1, at - 1 : at - 1 + CHUNK, :]
        total = total + cr[d, at + 1 : at + 1 + CHUNK, :] * field[d + 1, at + 1 : at + 1 + CHUNK, :]
        return (total - dg[d, c0 : c0 + CHUNK, :] * x) + sides, x

    def forward(n):
        def step(d, c0):
            rows = slice(c0, c0 + CHUNK)
            at = slice(PAD + c0, PAD + c0 + CHUNK)
            q, x = spread(pb.at[n + 1], d, c0)
            nxt = 2.0 * x - pb[n, d + 1, at, :] + wavelet[0, n] * sf[d, rows, :]
            nxt = nxt + kp[d, rows, :] * q

            def store():
                qb[n, d, rows, :] = q
                pb[n + 2, d + 1, at, :] = nxt

            return store

        return step

    def backward(n):
        m = NT - n

        def step(d, c0):
            rows = slice(c0, c0 + CHUNK)
            at = slice(PAD + c0, PAD + c0 + CHUNK)
            q, _ = spread(wb.at[m], d, c0)
            now = 2.0 * ab[m + 1, d, rows, :] - ab[m, d, rows, :]
            now = now + (kc[d, rows, :] * pb[n + 1, d + 1, at, :] - ob[n - 1, d, rows, :])
            now = now + q
            product = kp[d, rows, :] * now if n > 1 else None
            term = now * qb[n - 1, d, rows, :]
            if m > 0:
                term = gb[d, rows, :] + term

            def store():
                ab[m + 2, d, rows, :] = now
                if n > 1:
                    wb[m + 1, d + 1, at, :] = product
                gb[d, rows, :] = term

            return store

        return step

    def grad_copy(r, o, spot_rows):
        places = places_of(RETURNS[r])
        return remote(
            gc.at[places, spot_rows, :],
            gr.at[o, places],
            grad_send.at[r, o],
            grad_recv.at[r, o],
            half * 8 + peer(o),
            slab,
        )

    pieces = [[grad_copy(r, o, rows_of(peer(o))) for o in range(7)] for r in range(len(RETURNS))]
    merges = []
    for r, span in enumerate(RETURNS):
        places = places_of(span)
        merges.append(
            remote(
                acc.at[1 - half, places],
                pr.at[places],
                merge_send.at[r],
                merge_recv.at[r],
                partner,
                slab,
            )
        )

    def hand_in(r):
        low, high = RETURNS[r]
        width = high - low

        def wind(p, carry):
            values = unwind([gb[low + p], gb[depth - high + p]], col_anchor % ap, ap - row_anchor)
            gc[2 * low + p] = values[0]
            gc[2 * low + width + p] = values[1]
            return carry

        lax.fori_loop(0, width, wind, 0)
        for copy in pieces[r]:
            start_remote(copy)

    def collect(r):
        low, high = RETURNS[r]
        for copy in pieces[r]:
            finish_of(copy)

        def one(t, carry):
            sums = [jnp.zeros((own, ap), f32) for _ in range(4)]
            for o in range(8):
                value = gr[o, t] if o < 7 else gc[t, home, :]
                member = half * 8 + (origin(o) if o < 7 else lane_group)
                keep_row = my_rows >= anchors[0, member]
                keep_col = my_lanes >= anchors[1, member]
                top = jnp.where(keep_row, value, 0.0)
                bottom = jnp.where(keep_row, 0.0, value)
                sums[0] += jnp.where(keep_col, top, 0.0)
                sums[1] += jnp.where(keep_col, 0.0, top)
                sums[2] += jnp.where(keep_col, bottom, 0.0)
                sums[3] += jnp.where(keep_col, 0.0, bottom)
            acc[0, t, :, :ap] = sums[0]
            acc[0, t, :, ap:] = sums[1]
            acc[1, t, :, :ap] = sums[2]
            acc[1, t, :, ap:] = sums[3]
            return carry

        lax.fori_loop(2 * low, 2 * high, one, 0)
        start_remote(merges[r])

    def finish(r):
        low, high = RETURNS[r]
        finish_of(merges[r])

        def one(t, carry):
            pr[t] = pr[t] + acc[half, t]
            return carry

        lax.fori_loop(2 * low, 2 * high, one, 0)
        size = high - low
        for e in range(2):
            start_local(
                pltpu.make_async_copy(
                    pr.at[pl.ds(2 * low + e * size, size)],
                    grad_out.at[pl.ds(low if e == 0 else depth - high, size)],
                    out_sem.at[4 + 2 * r + e],
                )
            )

    for i in range(2, 6):
        finish_of(loads[i])
    settle(0)
    go(buoy_halo)
    settle(1)
    arrived(buoy_halo)
    arrived(wave_halo[0])
    each(0, 2, coefficients)
    each(0, 1, forward(0))
    go(wave_halo[1])
    each(1, 2, forward(0))
    go(back_halo[0])
    arrived(wave_halo[1])
    each(0, 1, forward(1))
    go(wave_halo[2])
    settle(2)
    each(2, 4, coefficients)
    each(2, 4, forward(0))
    each(1, 3, forward(1))
    arrived(wave_halo[2])
    each(0, 1, forward(2))
    go(wave_halo[3])
    each(1, 2, forward(2))
    arrived(back_halo[0])
    arrived(wave_halo[3])
    each(0, 1, forward(3))
    each(0, 1, backward(4))
    go(back_halo[1])
    settle(3)
    each(4, 8, coefficients)
    each(4, 8, forward(0))
    each(3, 4, forward(1))
    each(4, 8, forward(1))
    each(2, 8, forward(2))
    each(1, 2, forward(3))
    each(2, 8, forward(3))
    start_local(pltpu.make_async_copy(pb.at[NT, body, inner, :], wave_out.at[0, 0], out_sem.at[0]))
    start_local(pltpu.make_async_copy(pb.at[NT + 1, body, inner, :], wave_out.at[0, 1], out_sem.at[1]))
    each(1, 2, backward(4))
    each(2, 8, backward(4))
    arrived(back_halo[1])
    each(0, 1, backward(3))
    go(back_halo[2])
    each(1, 2, backward(3))
    each(2, 8, backward(3))
    each(1, 2, backward(2))
    each(2, 8, backward(2))
    each(4, 8, backward(1))
    hand_in(0)
    each(2, 4, backward(1))
    hand_in(1)
    arrived(back_halo[2])
    each(0, 1, backward(2))
    go(back_halo[3])
    start_local(pltpu.make_async_copy(ab.at[NT], adjoint_out.at[0, 0], out_sem.at[2]))
    each(1, 2, backward(1))
    hand_in(2)
    arrived(back_halo[3])
    each(0, 1, backward(1))
    hand_in(3)
    start_local(pltpu.make_async_copy(ab.at[NT + 1], adjoint_out.at[0, 1], out_sem.at[3]))
    collect(0)
    collect(1)
    collect(2)
    finish(0)
    collect(3)
    finish(1)
    finish(2)
    finish(3)
    for wait in sent:
        wait()
    for _, wait in due:
        wait()


def shards(
    kappa,
    buoyancy,
    anchors,
    wave_start,
    adjoint_start,
    wavelet,
    source_cell,
    receiver_cells,
    observed,
):
    depth, own, side = kappa.shape
    ap = wave_start.shape[3]
    count = receiver_cells.shape[1]
    parts = len(PARTS)
    f32 = jnp.float32
    any_space = pl.BlockSpec(memory_space=pl.ANY)
    smem = pl.BlockSpec(memory_space=pltpu.SMEM)
    vmem = pl.BlockSpec(memory_space=pltpu.VMEM)
    padded = (depth + 2, ap + 2 * PAD, ap)
    plain = (depth, ap, ap)
    return pl.pallas_call(
        kernel,
        out_shape=(
            jax.ShapeDtypeStruct(kappa.shape, f32),
            jax.ShapeDtypeStruct(wave_start.shape, f32),
            jax.ShapeDtypeStruct(adjoint_start.shape, f32),
        ),
        in_specs=[smem, smem, smem, any_space, any_space, any_space, any_space, vmem, vmem],
        out_specs=(any_space, any_space, any_space),
        scratch_shapes=[
            pltpu.VMEM((2, 2, depth, own, side), f32),
            pltpu.VMEM((7, depth, 2, own, ap), f32),
            pltpu.VMEM((depth, 2, ap, ap), f32),
            pltpu.VMEM((NT + 2,) + padded, f32),
            pltpu.VMEM((NT,) + plain, f32),
            pltpu.VMEM(plain, f32),
            pltpu.VMEM(padded, f32),
            pltpu.VMEM((depth + 1, ap, ap), f32),
            pltpu.VMEM((depth, ap + 2 * PAD, ap), f32),
            pltpu.VMEM(plain, f32),
            pltpu.VMEM(plain, f32),
            pltpu.VMEM((NT,) + padded, f32),
            pltpu.VMEM((NT + 2,) + plain, f32),
            pltpu.VMEM(plain, f32),
            pltpu.VMEM((NT,) + plain, f32),
            pltpu.VMEM(plain, f32),
            pltpu.VMEM((13 * ap, count), jnp.bfloat16),
            pltpu.VMEM(plain, f32),
            pltpu.VMEM(plain, f32),
            pltpu.VMEM((7, depth, own, ap), f32),
            pltpu.VMEM((2, depth, own, side), f32),
            pltpu.VMEM((depth, own, side), f32),
            pltpu.VMEM((4, 2 * ap, ap), f32),
            pltpu.SemaphoreType.DMA((6,)),
            pltpu.SemaphoreType.DMA((parts, 2, 2)),
            pltpu.SemaphoreType.DMA((parts, 2, 2)),
            pltpu.SemaphoreType.DMA((parts, 7)),
            pltpu.SemaphoreType.DMA((parts, 7)),
            pltpu.SemaphoreType.DMA((2 * NT + 1, 2)),
            pltpu.SemaphoreType.DMA((2 * NT + 1, 2)),
            pltpu.SemaphoreType.DMA((len(RETURNS), 7)),
            pltpu.SemaphoreType.DMA((len(RETURNS), 7)),
            pltpu.SemaphoreType.DMA((len(RETURNS),)),
            pltpu.SemaphoreType.DMA((len(RETURNS),)),
            pltpu.SemaphoreType.DMA((4 + 2 * len(RETURNS),)),
        ],
        compiler_params=pltpu.CompilerParams(
            collective_id=0, has_side_effects=True, vmem_limit_bytes=60 * 1024 * 1024
        ),
    )(
        anchors.T,
        wavelet,
        source_cell,
        kappa,
        buoyancy,
        wave_start,
        adjoint_start,
        jnp.transpose(receiver_cells, (2, 0, 1)),
        observed[0],
    )


def solution(mesh):
    in_specs = (
        P("slab", "shot", None),
        P("slab", "shot", None),
        P(),
        P("shot", None, "slab", None, None),
        P("shot", None, "slab", None, None),
        P("shot", None),
        P("shot", None),
        P("shot", None, None),
        P("shot", None, None),
    )
    out_specs = (
        P("slab", "shot", None),
        P("shot", None, "slab", None, None),
        P("shot", None, "slab", None, None),
    )
    return jax.shard_map(shards, mesh=mesh, in_specs=in_specs, out_specs=out_specs, check_vma=False)
```

```python
import jax
import jax.numpy as jnp
from jax import lax
from jax.experimental import pallas as pl
from jax.experimental.pallas import tpu as pltpu
from jax.sharding import PartitionSpec as P

MESH = pl.DeviceIdType.MESH
NT = 4
PAD = 8
CHUNK = 128
PARTS = ((0, 1), (1, 3), (3, 5), (5, 8))
RETURNS = ((4, 8), (2, 4), (1, 2), (0, 1))
OFFSETS = ((2, 0), (2, 1), (1, 0), (3, 0), (1, 1), (3, 1), (0, 1))


def kernel(
    anchors,
    wavelet,
    source,
    kappa,
    buoyancy,
    wave,
    adjoint,
    cells,
    observed,
    grad_out,
    wave_out,
    adjoint_out,
    raw,
    pack,
    win,
    pb,
    qb,
    kp,
    bz,
    fd,
    cr,
    cc,
    dg,
    wb,
    ab,
    kc,
    ob,
    sf,
    vb,
    gb,
    gc,
    gr,
    acc,
    pr,
    tmp,
    load_sem,
    swap_send,
    swap_recv,
    win_send,
    win_recv,
    halo_send,
    halo_recv,
    grad_send,
    grad_recv,
    merge_send,
    merge_recv,
    out_sem,
):
    depth, own, side = kappa.shape
    ap = side // 2
    f32 = jnp.float32
    shot = lax.axis_index("shot")
    slab = lax.axis_index("slab")
    slabs = lax.axis_size("slab")
    half = shot // 8
    lane_group = shot % 8
    px = lane_group // 2
    pc = lane_group % 2
    partner = (shot + 8) % 16
    below = (slab + 1) % slabs
    above = (slab + slabs - 1) % slabs

    def peer(o):
        dx, dc = OFFSETS[o]
        return ((px + dx) % 4) * 2 + (pc + dc) % 2

    def origin(o):
        dx, dc = OFFSETS[o]
        return ((px + 4 - dx) % 4) * 2 + (pc + 2 - dc) % 2

    sent = []
    due = []

    def start_local(copy):
        copy.start()
        due.append((copy, copy.wait))

    def start_remote(copy):
        copy.start()
        sent.append(copy.wait_send)
        due.append((copy, copy.wait_recv))

    def finish_of(copy):
        for i, (known, wait) in enumerate(due):
            if known is copy or (isinstance(copy, tuple) and known == copy):
                due.pop(i)
                wait()
                return
        raise ValueError(copy)

    def remote(src, dst, send, recv, to_shot, to_slab):
        return pltpu.make_async_remote_copy(
            src_ref=src,
            dst_ref=dst,
            send_sem=send,
            recv_sem=recv,
            device_id={"shot": to_shot, "slab": to_slab},
            device_id_type=MESH,
        )

    inner = pl.ds(PAD, ap)
    body = pl.ds(1, depth)

    barrier = pltpu.get_barrier_semaphore()

    def greet(to_shot, to_slab):
        pl.semaphore_signal(
            barrier, inc=1, device_id={"shot": to_shot, "slab": to_slab}, device_id_type=MESH
        )

    greet(partner, slab)
    greet(shot, below)
    greet(shot, above)
    for o in range(7):
        greet(half * 8 + peer(o), slab)

    loads = [
        pltpu.make_async_copy(buoyancy, raw.at[half, 0], load_sem.at[0]),
        pltpu.make_async_copy(kappa, raw.at[half, 1], load_sem.at[1]),
        pltpu.make_async_copy(wave.at[0, 0], pb.at[0, body, inner, :], load_sem.at[2]),
        pltpu.make_async_copy(wave.at[0, 1], pb.at[1, body, inner, :], load_sem.at[3]),
        pltpu.make_async_copy(adjoint.at[0, 0], ab.at[0], load_sem.at[4]),
        pltpu.make_async_copy(adjoint.at[0, 1], ab.at[1], load_sem.at[5]),
    ]
    for copy in loads:
        start_local(copy)

    margin = jnp.zeros((PAD, ap), f32)

    def clear(i, carry):
        for n in range(NT):
            pb[n + 1, i + 1, :PAD, :] = margin
            pb[n + 1, i + 1, PAD + ap :, :] = margin
            wb[n, i + 1, :PAD, :] = margin
            wb[n, i + 1, PAD + ap :, :] = margin
        bz[i + 1, :PAD, :] = margin
        bz[i + 1, PAD + ap :, :] = margin
        cr[i, PAD + ap :, :] = margin
        return carry

    lax.fori_loop(0, depth, clear, 0)

    count = cells.shape[2]
    rows_at = lax.broadcasted_iota(jnp.int32, (ap, ap), 0)
    lanes_at = lax.broadcasted_iota(jnp.int32, (ap, ap), 1)
    flat = (cells[0] - slab * depth) * ap + cells[1]
    upright = jnp.concatenate(
        [cells[2].astype(f32), observed[...], jnp.zeros((7 - NT, count), f32)], axis=0
    ).T
    hit = lax.broadcasted_iota(jnp.int32, (count, ap), 1).astype(f32) == upright[:, :1]

    for n in range(NT):
        rest = jnp.where(hit, upright[:, n + 1 : n + 2], 0.0)
        base = (n // 2) * 6 * ap + (n % 2) * ap
        for part in range(3):
            top = rest.astype(jnp.bfloat16)
            vb[:, base + part * 2 * ap : base + (part * 2 + 1) * ap] = top
            rest = rest - top.astype(f32)
    vb[:, 12 * ap :] = jnp.where(hit, 1.0, 0.0).astype(jnp.bfloat16)

    def mark(d, carry):
        here = (rows_at == source[0, 1]) & (lanes_at == source[0, 2])
        deep = jnp.where(source[0, 0] == slab * depth + d, 1.0, 0.0)
        sf[d, :, :] = jnp.where(here, deep, 0.0)
        return carry

    lax.fori_loop(0, depth, mark, 0)

    group = 4

    def spot(ch):
        at = lax.broadcasted_iota(jnp.int32, (group * ap, count), 0) + ch * (group * ap)
        onehot = jnp.where(flat == at, 1.0, 0.0).astype(jnp.bfloat16)

        def times(row, width):
            return lax.dot_general(
                onehot, vb[:, row : row + width], (((1,), (0,)), ((), ())), preferred_element_type=f32
            )

        for pair in range(NT // 2):
            total = times(pair * 6 * ap, 2 * ap)
            total = total + times(pair * 6 * ap + 2 * ap, 2 * ap)
            total = total + times(pair * 6 * ap + 4 * ap, 2 * ap)
            total = total.reshape(group, ap, 2 * ap)
            ob[2 * pair, pl.ds(ch * group, group), :, :] = total[:, :, :ap]
            ob[2 * pair + 1, pl.ds(ch * group, group), :, :] = total[:, :, ap:]
        kc[pl.ds(ch * group, group), :, :] = times(12 * ap, ap).reshape(group, ap, ap)

    for ch in range(depth // group):
        spot(ch)
    pl.semaphore_wait(barrier, 10)

    def plane_of(span, p):
        low, high = span
        width = high - low
        return low + p + (p // width) * (depth - high - low - width)

    def places_of(span):
        low, high = span
        return pl.ds(2 * low, 2 * (high - low))

    swaps = []
    for q, (low, high) in enumerate(PARTS):
        swaps.append([])
        for i, ref in enumerate((buoyancy, kappa)):
            for e in range(2):
                planes = pl.ds(low if e == 0 else depth - high, high - low)
                swaps[q].append(
                    remote(
                        ref.at[planes],
                        raw.at[half, i, planes],
                        swap_send.at[q, i, e],
                        swap_recv.at[q, i, e],
                        partner,
                        slab,
                    )
                )

    def swap_part(q):
        for copy in swaps[q]:
            start_remote(copy)

    def field_halo(slot, field, src=None):
        first = field.at[1, inner, :] if src is None else src.at[0]
        last = field.at[depth, inner, :] if src is None else src.at[depth - 1]
        return (
            remote(
                first,
                field.at[depth + 1, inner, :],
                halo_send.at[slot, 0],
                halo_recv.at[slot, 0],
                shot,
                above,
            ),
            remote(
                last,
                field.at[0, inner, :],
                halo_send.at[slot, 1],
                halo_recv.at[slot, 1],
                shot,
                below,
            ),
        )

    wave_halo = [field_halo(0, pb.at[1], wave.at[0, 1])]
    wave_halo += [field_halo(n, pb.at[n + 1]) for n in range(1, NT)]
    back_halo = [field_halo(NT + m, wb.at[m]) for m in range(NT)]
    buoy_halo = field_halo(2 * NT, bz)

    def go(pair):
        start_remote(pair[0])
        start_remote(pair[1])

    def arrived(pair):
        finish_of(pair[0])
        finish_of(pair[1])

    swap_part(0)
    swap_part(1)

    my_rows = lax.broadcasted_iota(jnp.int32, (own, ap), 0) + lane_group * own
    my_lanes = lax.broadcasted_iota(jnp.int32, (own, ap), 1)

    def rows_of(member):
        return pl.ds(pl.multiple_of(member * own, own), own)

    home = rows_of(lane_group)

    def window_copy(q, o, spot_rows):
        return remote(
            pack.at[o, places_of(PARTS[q])],
            win.at[places_of(PARTS[q]), :, spot_rows, :],
            win_send.at[q, o],
            win_recv.at[q, o],
            half * 8 + peer(o),
            slab,
        )

    finish_of(loads[0])
    finish_of(loads[1])
    def pack_part(q):
        part = PARTS[q]
        for copy in swaps[q]:
            finish_of(copy)

        def fill(p, carry):
            d = plane_of(part, p)
            t = 2 * part[0] + p
            for i in range(2):
                low = raw[0, i, d]
                high = raw[1, i, d]
                for o in range(8):
                    member = half * 8 + (peer(o) if o < 7 else lane_group)
                    keep_row = my_rows >= anchors[0, member]
                    keep_col = my_lanes >= anchors[1, member]
                    a = jnp.where(keep_col, low[:, :ap], low[:, ap:])
                    b = jnp.where(keep_col, high[:, :ap], high[:, ap:])
                    value = jnp.where(keep_row, a, b)
                    if o < 7:
                        pack[o, t, i] = value
                    else:
                        win[t, i, home, :] = value
            return carry

        lax.fori_loop(0, 2 * (part[1] - part[0]), fill, 0)

    def send_part(q):
        for o in range(7):
            copy = window_copy(q, o, home)
            copy.start()
            due.append(((q, o, "sent"), copy.wait_send))
            landing = window_copy(q, o, rows_of(origin(o)))
            due.append(((q, o), landing.wait_recv))

    def sent_part(q):
        for o in range(7):
            finish_of((q, o, "sent"))

    row_anchor = anchors[0, shot]
    col_anchor = anchors[1, shot]

    def unwind(values, lane_shift, first_row):
        for t, x in enumerate(values):
            x = pltpu.roll(x, lane_shift, axis=1)
            tmp[t, :ap, :] = x
            tmp[t, ap:, :] = x
        return [tmp[t, pl.ds(first_row, ap), :] for t in range(len(values))]

    lane_back = (ap - col_anchor) % ap

    def settle(q):
        low, high = PARTS[q]
        width = high - low
        for o in range(7):
            finish_of((q, o))

        def one(p, carry):
            t = 2 * low + p
            values = [win[t, 0], win[t, 1], win[t + width, 0], win[t + width, 1]]
            values = unwind(values, lane_back, row_anchor)
            products = []
            for e in range(2):
                d = low + p if e == 0 else depth - high + p
                products.append(values[2 * e + 1] * ab[1, d])
            for e in range(2):
                d = low + p if e == 0 else depth - high + p
                bz[d + 1, inner, :] = values[2 * e]
                kp[d] = values[2 * e + 1]
                wb[0, d + 1, inner, :] = products[e]
            return carry

        lax.fori_loop(0, width, one, 0)

    def each(low, high, step):
        pairs = 2 if (high - low) % 2 == 0 else 1

        def some(i, carry):
            layers = []
            for t in range(pairs):
                d = low + i * pairs + t
                layers += [d, depth - 1 - d]
            for c0 in range(0, ap, CHUNK):
                stores = [step(d, c0) for d in layers]
                for store in stores:
                    store()
            return carry

        lax.fori_loop(0, (high - low) // pairs, some, 0)

    def coefficients(d, c0):
        first = (slab == 0) & (d == 0)
        last = (slab == slabs - 1) & (d == depth - 1)
        rows = lax.broadcasted_iota(jnp.int32, (CHUNK, ap), 0) + c0
        lanes = lax.broadcasted_iota(jnp.int32, (CHUNK, ap), 1)
        at = slice(PAD + c0, PAD + c0 + CHUNK)
        x = bz[d + 1, at, :]
        prev = bz[d + 1, PAD + c0 - 1 : PAD + c0 - 1 + CHUNK, :]
        succ = bz[d + 1, PAD + c0 + 1 : PAD + c0 + 1 + CHUNK, :]
        across = 0.5 * (x + prev)
        total = across + 0.5 * (x + succ)
        across = jnp.where(rows == 0, 0.0, across)
        prev = jnp.where(lanes == 0, 0.0, pltpu.roll(x, 1, axis=1))
        succ = jnp.where(lanes == ap - 1, 0.0, pltpu.roll(x, ap - 1, axis=1))
        along = 0.5 * (x + prev)
        total = total + along + 0.5 * (x + succ)
        along = jnp.where(lanes == 0, 0.0, along)
        low = 0.5 * (x + jnp.where(first, 0.0, bz[d, at, :]))
        high = 0.5 * (x + jnp.where(last, 0.0, bz[d + 2, at, :]))
        total = total + low + high
        low = jnp.where(first, 0.0, low)
        high = jnp.where(last, 0.0, high)

        def store():
            cr[d, at, :] = across
            cc[d, c0 : c0 + CHUNK, :] = along
            fd[d, c0 : c0 + CHUNK, :] = low
            fd[d + 1, c0 : c0 + CHUNK, :] = high
            dg[d, c0 : c0 + CHUNK, :] = total

        return store

    def spread(field, d, c0):
        at = PAD + c0
        x = field[d + 1, at : at + CHUNK, :]
        across = cc[d, c0 : c0 + CHUNK, :]
        sides = across * pltpu.roll(x, 1, axis=1)
        sides = sides + pltpu.roll(across * x, ap - 1, axis=1)
        total = fd[d, c0 : c0 + CHUNK, :] * field[d, at : at + CHUNK, :]
        total = total + fd[d + 1, c0 : c0 + CHUNK, :] * field[d + 2, at : at + CHUNK, :]
        total = total + cr[d, at : at + CHUNK, :] * field[d + 1, at - 1 : at - 1 + CHUNK, :]
        total = total + cr[d, at + 1 : at + 1 + CHUNK, :] * field[d + 1, at + 1 : at + 1 + CHUNK, :]
        return (total - dg[d, c0 : c0 + CHUNK, :] * x) + sides, x

    def forward(n):
        def step(d, c0):
            rows = slice(c0, c0 + CHUNK)
            at = slice(PAD + c0, PAD + c0 + CHUNK)
            q, x = spread(pb.at[n + 1], d, c0)
            nxt = 2.0 * x - pb[n, d + 1, at, :] + wavelet[0, n] * sf[d, rows, :]
            nxt = nxt + kp[d, rows, :] * q

            def store():
                qb[n, d, rows, :] = q
                pb[n + 2, d + 1, at, :] = nxt

            return store

        return step

    def backward(n):
        m = NT - n

        def step(d, c0):
            rows = slice(c0, c0 + CHUNK)
            at = slice(PAD + c0, PAD + c0 + CHUNK)
            q, _ = spread(wb.at[m], d, c0)
            now = 2.0 * ab[m + 1, d, rows, :] - ab[m, d, rows, :]
            now = now + (kc[d, rows, :] * pb[n + 1, d + 1, at, :] - ob[n - 1, d, rows, :])
            now = now + q
            product = kp[d, rows, :] * now if n > 1 else None
            term = now * qb[n - 1, d, rows, :]
            if m > 0:
                term = gb[d, rows, :] + term

            def store():
                ab[m + 2, d, rows, :] = now
                if n > 1:
                    wb[m + 1, d + 1, at, :] = product
                gb[d, rows, :] = term

            return store

        return step

    def grad_copy(r, o, spot_rows):
        places = places_of(RETURNS[r])
        return remote(
            gc.at[places, spot_rows, :],
            gr.at[o, places],
            grad_send.at[r, o],
            grad_recv.at[r, o],
            half * 8 + peer(o),
            slab,
        )

    pieces = [[grad_copy(r, o, rows_of(peer(o))) for o in range(7)] for r in range(len(RETURNS))]
    merges = []
    for r, span in enumerate(RETURNS):
        places = places_of(span)
        merges.append(
            remote(
                acc.at[1 - half, places],
                pr.at[places],
                merge_send.at[r],
                merge_recv.at[r],
                partner,
                slab,
            )
        )

    def hand_in(r):
        low, high = RETURNS[r]
        width = high - low

        def wind(p, carry):
            values = unwind([gb[low + p], gb[depth - high + p]], col_anchor % ap, ap - row_anchor)
            gc[2 * low + p] = values[0]
            gc[2 * low + width + p] = values[1]
            return carry

        lax.fori_loop(0, width, wind, 0)
        for copy in pieces[r]:
            start_remote(copy)

    def collect(r):
        low, high = RETURNS[r]
        for copy in pieces[r]:
            finish_of(copy)

        def one(t, carry):
            sums = [jnp.zeros((own, ap), f32) for _ in range(4)]
            for o in range(8):
                value = gr[o, t] if o < 7 else gc[t, home, :]
                member = half * 8 + (origin(o) if o < 7 else lane_group)
                keep_row = my_rows >= anchors[0, member]
                keep_col = my_lanes >= anchors[1, member]
                top = jnp.where(keep_row, value, 0.0)
                bottom = jnp.where(keep_row, 0.0, value)
                sums[0] += jnp.where(keep_col, top, 0.0)
                sums[1] += jnp.where(keep_col, 0.0, top)
                sums[2] += jnp.where(keep_col, bottom, 0.0)
                sums[3] += jnp.where(keep_col, 0.0, bottom)
            acc[0, t, :, :ap] = sums[0]
            acc[0, t, :, ap:] = sums[1]
            acc[1, t, :, :ap] = sums[2]
            acc[1, t, :, ap:] = sums[3]
            return carry

        lax.fori_loop(2 * low, 2 * high, one, 0)
        start_remote(merges[r])

    def finish(r):
        low, high = RETURNS[r]
        finish_of(merges[r])

        def one(t, carry):
            pr[t] = pr[t] + acc[half, t]
            return carry

        lax.fori_loop(2 * low, 2 * high, one, 0)
        size = high - low
        for e in range(2):
            start_local(
                pltpu.make_async_copy(
                    pr.at[pl.ds(2 * low + e * size, size)],
                    grad_out.at[pl.ds(low if e == 0 else depth - high, size)],
                    out_sem.at[4 + 2 * r + e],
                )
            )

    pack_part(0)
    send_part(0)
    swap_part(2)
    pack_part(1)
    send_part(1)
    swap_part(3)
    go(wave_halo[0])
    pack_part(2)
    send_part(2)
    for i in range(2, 6):
        finish_of(loads[i])
    settle(0)
    go(buoy_halo)
    pack_part(3)
    sent_part(1)
    send_part(3)
    arrived(wave_halo[0])
    settle(1)
    arrived(buoy_halo)
    each(0, 2, coefficients)
    each(0, 1, forward(0))
    go(wave_halo[1])
    each(1, 2, forward(0))
    go(back_halo[0])
    arrived(wave_halo[1])
    each(0, 1, forward(1))
    go(wave_halo[2])
    settle(2)
    each(2, 4, coefficients)
    each(2, 4, forward(0))
    each(1, 3, forward(1))
    arrived(wave_halo[2])
    each(0, 1, forward(2))
    go(wave_halo[3])
    each(1, 2, forward(2))
    settle(3)
    each(4, 8, coefficients)
    arrived(back_halo[0])
    arrived(wave_halo[3])
    each(0, 1, forward(3))
    each(0, 1, backward(4))
    go(back_halo[1])
    each(4, 8, forward(0))
    each(3, 4, forward(1))
    each(4, 8, forward(1))
    each(2, 4, forward(2))
    each(4, 8, forward(2))
    each(1, 2, forward(3))
    each(1, 2, backward(4))
    each(2, 8, forward(3))
    start_local(pltpu.make_async_copy(pb.at[NT, body, inner, :], wave_out.at[0, 0], out_sem.at[0]))
    start_local(pltpu.make_async_copy(pb.at[NT + 1, body, inner, :], wave_out.at[0, 1], out_sem.at[1]))
    arrived(back_halo[1])
    each(0, 1, backward(3))
    go(back_halo[2])
    each(2, 8, backward(4))
    each(1, 2, backward(3))
    each(2, 8, backward(3))
    each(1, 2, backward(2))
    each(2, 8, backward(2))
    each(4, 8, backward(1))
    hand_in(0)
    each(2, 4, backward(1))
    hand_in(1)
    arrived(back_halo[2])
    each(0, 1, backward(2))
    go(back_halo[3])
    start_local(pltpu.make_async_copy(ab.at[NT], adjoint_out.at[0, 0], out_sem.at[2]))
    each(1, 2, backward(1))
    hand_in(2)
    arrived(back_halo[3])
    each(0, 1, backward(1))
    hand_in(3)
    start_local(pltpu.make_async_copy(ab.at[NT + 1], adjoint_out.at[0, 1], out_sem.at[3]))
    collect(0)
    collect(1)
    collect(2)
    finish(0)
    collect(3)
    finish(1)
    finish(2)
    finish(3)
    for wait in sent:
        wait()
    for _, wait in due:
        wait()


def deliver(grad, wave, adjoint, grad_out, wave_out, adjoint_out, sem):
    copies = [pltpu.make_async_copy(grad, grad_out, sem.at[0])]
    for e in range(2):
        copies.append(pltpu.make_async_copy(wave.at[0, e], wave_out.at[0, e], sem.at[1 + e]))
        copies.append(pltpu.make_async_copy(adjoint.at[0, e], adjoint_out.at[0, e], sem.at[3 + e]))
    for copy in copies:
        copy.start()
    for copy in copies:
        copy.wait()


def shards(
    kappa,
    buoyancy,
    anchors,
    wave_start,
    adjoint_start,
    wavelet,
    source_cell,
    receiver_cells,
    observed,
):
    depth, own, side = kappa.shape
    ap = wave_start.shape[3]
    count = receiver_cells.shape[1]
    parts = len(PARTS)
    f32 = jnp.float32
    any_space = pl.BlockSpec(memory_space=pl.ANY)
    smem = pl.BlockSpec(memory_space=pltpu.SMEM)
    vmem = pl.BlockSpec(memory_space=pltpu.VMEM)
    padded = (depth + 2, ap + 2 * PAD, ap)
    plain = (depth, ap, ap)
    results = pl.pallas_call(
        kernel,
        out_shape=(
            pltpu.VMEM(kappa.shape, f32),
            pltpu.VMEM(wave_start.shape, f32),
            pltpu.VMEM(adjoint_start.shape, f32),
        ),
        in_specs=[smem, smem, smem, any_space, any_space, any_space, any_space, vmem, vmem],
        out_specs=(any_space, any_space, any_space),
        scratch_shapes=[
            pltpu.VMEM((2, 2, depth, own, side), f32),
            pltpu.VMEM((7, depth, 2, own, ap), f32),
            pltpu.VMEM((depth, 2, ap, ap), f32),
            pltpu.VMEM((NT + 2,) + padded, f32),
            pltpu.VMEM((NT,) + plain, f32),
            pltpu.VMEM(plain, f32),
            pltpu.VMEM(padded, f32),
            pltpu.VMEM((depth + 1, ap, ap), f32),
            pltpu.VMEM((depth, ap + 2 * PAD, ap), f32),
            pltpu.VMEM(plain, f32),
            pltpu.VMEM(plain, f32),
            pltpu.VMEM((NT,) + padded, f32),
            pltpu.VMEM((NT + 2,) + plain, f32),
            pltpu.VMEM(plain, f32),
            pltpu.VMEM((NT,) + plain, f32),
            pltpu.VMEM(plain, f32),
            pltpu.VMEM((count, 13 * ap), jnp.bfloat16),
            pltpu.VMEM(plain, f32),
            pltpu.VMEM(plain, f32),
            pltpu.VMEM((7, depth, own, ap), f32),
            pltpu.VMEM((2, depth, own, side), f32),
            pltpu.VMEM((depth, own, side), f32),
            pltpu.VMEM((4, 2 * ap, ap), f32),
            pltpu.SemaphoreType.DMA((6,)),
            pltpu.SemaphoreType.DMA((parts, 2, 2)),
            pltpu.SemaphoreType.DMA((parts, 2, 2)),
            pltpu.SemaphoreType.DMA((parts, 7)),
            pltpu.SemaphoreType.DMA((parts, 7)),
            pltpu.SemaphoreType.DMA((2 * NT + 1, 2)),
            pltpu.SemaphoreType.DMA((2 * NT + 1, 2)),
            pltpu.SemaphoreType.DMA((len(RETURNS), 7)),
            pltpu.SemaphoreType.DMA((len(RETURNS), 7)),
            pltpu.SemaphoreType.DMA((len(RETURNS),)),
            pltpu.SemaphoreType.DMA((len(RETURNS),)),
            pltpu.SemaphoreType.DMA((4 + 2 * len(RETURNS),)),
        ],
        compiler_params=pltpu.CompilerParams(
            collective_id=0, has_side_effects=True, vmem_limit_bytes=57 * 1024 * 1024
        ),
    )(
        anchors.T,
        wavelet,
        source_cell,
        kappa,
        buoyancy,
        wave_start,
        adjoint_start,
        jnp.transpose(receiver_cells, (2, 0, 1)),
        observed[0],
    )
    return results


def solution(mesh):
    in_specs = (
        P("slab", "shot", None),
        P("slab", "shot", None),
        P(),
        P("shot", None, "slab", None, None),
        P("shot", None, "slab", None, None),
        P("shot", None),
        P("shot", None),
        P("shot", None, None),
        P("shot", None, None),
    )
    out_specs = (
        P("slab", "shot", None),
        P("shot", None, "slab", None, None),
        P("shot", None, "slab", None, None),
    )
    return jax.shard_map(shards, mesh=mesh, in_specs=in_specs, out_specs=out_specs, check_vma=False)
```

```python
import jax
import jax.numpy as jnp
from jax import lax
from jax.experimental import pallas as pl
from jax.experimental.pallas import tpu as pltpu
from jax.sharding import PartitionSpec as P

MESH = pl.DeviceIdType.MESH
NT = 4
PAD = 8
CHUNK = 128
PARTS = ((0, 1), (1, 3), (3, 5), (5, 8))
RETURNS = ((4, 8), (2, 4), (1, 2), (0, 1))
OFFSETS = ((2, 0), (2, 1), (1, 0), (3, 0), (1, 1), (3, 1), (0, 1))


def kernel(
    anchors,
    wavelet,
    source,
    kappa,
    buoyancy,
    wave,
    adjoint,
    cells,
    observed,
    grad_out,
    wave_out,
    adjoint_out,
    raw,
    pack,
    win,
    pb,
    qb,
    kp,
    bz,
    fd,
    cr,
    cc,
    dg,
    wb,
    ab,
    kc,
    ob,
    sf,
    vb,
    gb,
    gc,
    gr,
    acc,
    pr,
    tmp,
    load_sem,
    swap_send,
    swap_recv,
    win_send,
    win_recv,
    halo_send,
    halo_recv,
    grad_send,
    grad_recv,
    merge_send,
    merge_recv,
    out_sem,
):
    depth, own, side = kappa.shape
    ap = side // 2
    f32 = jnp.float32
    shot = lax.axis_index("shot")
    slab = lax.axis_index("slab")
    slabs = lax.axis_size("slab")
    half = shot // 8
    lane_group = shot % 8
    px = lane_group // 2
    pc = lane_group % 2
    partner = (shot + 8) % 16
    below = (slab + 1) % slabs
    above = (slab + slabs - 1) % slabs

    def peer(o):
        dx, dc = OFFSETS[o]
        return ((px + dx) % 4) * 2 + (pc + dc) % 2

    def origin(o):
        dx, dc = OFFSETS[o]
        return ((px + 4 - dx) % 4) * 2 + (pc + 2 - dc) % 2

    sent = []
    due = []

    def start_local(copy):
        copy.start()
        due.append((copy, copy.wait))

    def start_remote(copy):
        copy.start()
        sent.append(copy.wait_send)
        due.append((copy, copy.wait_recv))

    def finish_of(copy):
        for i, (known, wait) in enumerate(due):
            if known is copy or (isinstance(copy, tuple) and known == copy):
                due.pop(i)
                wait()
                return
        raise ValueError(copy)

    def remote(src, dst, send, recv, to_shot, to_slab):
        return pltpu.make_async_remote_copy(
            src_ref=src,
            dst_ref=dst,
            send_sem=send,
            recv_sem=recv,
            device_id={"shot": to_shot, "slab": to_slab},
            device_id_type=MESH,
        )

    inner = pl.ds(PAD, ap)
    body = pl.ds(1, depth)

    barrier = pltpu.get_barrier_semaphore()

    def greet(to_shot, to_slab):
        pl.semaphore_signal(
            barrier, inc=1, device_id={"shot": to_shot, "slab": to_slab}, device_id_type=MESH
        )

    greet(partner, slab)
    greet(shot, below)
    greet(shot, above)
    for o in range(7):
        greet(half * 8 + peer(o), slab)

    loads = [
        pltpu.make_async_copy(buoyancy, raw.at[half, 0], load_sem.at[0]),
        pltpu.make_async_copy(kappa, raw.at[half, 1], load_sem.at[1]),
        pltpu.make_async_copy(wave.at[0, 0], pb.at[0, body, inner, :], load_sem.at[2]),
        pltpu.make_async_copy(wave.at[0, 1], pb.at[1, body, inner, :], load_sem.at[3]),
        pltpu.make_async_copy(adjoint.at[0, 0], ab.at[0], load_sem.at[4]),
        pltpu.make_async_copy(adjoint.at[0, 1], ab.at[1], load_sem.at[5]),
    ]
    for copy in loads:
        start_local(copy)

    margin = jnp.zeros((PAD, ap), f32)

    def clear(i, carry):
        for n in range(NT):
            pb[n + 1, i + 1, :PAD, :] = margin
            pb[n + 1, i + 1, PAD + ap :, :] = margin
            wb[n, i + 1, :PAD, :] = margin
            wb[n, i + 1, PAD + ap :, :] = margin
        bz[i + 1, :PAD, :] = margin
        bz[i + 1, PAD + ap :, :] = margin
        cr[i, PAD + ap :, :] = margin
        return carry

    lax.fori_loop(0, depth, clear, 0)

    count = cells.shape[2]
    rows_at = lax.broadcasted_iota(jnp.int32, (ap, ap), 0)
    lanes_at = lax.broadcasted_iota(jnp.int32, (ap, ap), 1)
    flat = (cells[0] - slab * depth) * ap + cells[1]
    upright = jnp.concatenate(
        [cells[2].astype(f32), observed[...], jnp.zeros((7 - NT, count), f32)], axis=0
    ).T
    hit = lax.broadcasted_iota(jnp.int32, (count, ap), 1).astype(f32) == upright[:, :1]

    for n in range(NT):
        rest = jnp.where(hit, upright[:, n + 1 : n + 2], 0.0)
        base = (n // 2) * 6 * ap + (n % 2) * ap
        for part in range(3):
            top = rest.astype(jnp.bfloat16)
            vb[:, base + part * 2 * ap : base + (part * 2 + 1) * ap] = top
            rest = rest - top.astype(f32)
    vb[:, 12 * ap :] = jnp.where(hit, 1.0, 0.0).astype(jnp.bfloat16)

    def mark(d, carry):
        here = (rows_at == source[0, 1]) & (lanes_at == source[0, 2])
        deep = jnp.where(source[0, 0] == slab * depth + d, 1.0, 0.0)
        sf[d, :, :] = jnp.where(here, deep, 0.0)
        return carry

    lax.fori_loop(0, depth, mark, 0)

    group = 4

    def spot(ch):
        at = lax.broadcasted_iota(jnp.int32, (group * ap, count), 0) + ch * (group * ap)
        onehot = jnp.where(flat == at, 1.0, 0.0).astype(jnp.bfloat16)

        def times(row, width):
            return lax.dot_general(
                onehot, vb[:, row : row + width], (((1,), (0,)), ((), ())), preferred_element_type=f32
            )

        for pair in range(NT // 2):
            total = times(pair * 6 * ap, 2 * ap)
            total = total + times(pair * 6 * ap + 2 * ap, 2 * ap)
            total = total + times(pair * 6 * ap + 4 * ap, 2 * ap)
            total = total.reshape(group, ap, 2 * ap)
            ob[2 * pair, pl.ds(ch * group, group), :, :] = total[:, :, :ap]
            ob[2 * pair + 1, pl.ds(ch * group, group), :, :] = total[:, :, ap:]
        kc[pl.ds(ch * group, group), :, :] = times(12 * ap, ap).reshape(group, ap, ap)

    pl.semaphore_wait(barrier, 10)

    def plane_of(span, p):
        low, high = span
        width = high - low
        return low + p + (p // width) * (depth - high - low - width)

    def places_of(span):
        low, high = span
        return pl.ds(2 * low, 2 * (high - low))

    swaps = []
    for q, (low, high) in enumerate(PARTS):
        swaps.append([])
        for i, ref in enumerate((buoyancy, kappa)):
            for e in range(2):
                planes = pl.ds(low if e == 0 else depth - high, high - low)
                swaps[q].append(
                    remote(
                        ref.at[planes],
                        raw.at[half, i, planes],
                        swap_send.at[q, i, e],
                        swap_recv.at[q, i, e],
                        partner,
                        slab,
                    )
                )

    def swap_part(q):
        for copy in swaps[q]:
            start_remote(copy)

    def field_halo(slot, field, src=None):
        first = field.at[1, inner, :] if src is None else src.at[0]
        last = field.at[depth, inner, :] if src is None else src.at[depth - 1]
        return (
            remote(
                first,
                field.at[depth + 1, inner, :],
                halo_send.at[slot, 0],
                halo_recv.at[slot, 0],
                shot,
                above,
            ),
            remote(
                last,
                field.at[0, inner, :],
                halo_send.at[slot, 1],
                halo_recv.at[slot, 1],
                shot,
                below,
            ),
        )

    wave_halo = [field_halo(0, pb.at[1], wave.at[0, 1])]
    wave_halo += [field_halo(n, pb.at[n + 1]) for n in range(1, NT)]
    back_halo = [field_halo(NT + m, wb.at[m]) for m in range(NT)]
    buoy_halo = field_halo(2 * NT, bz)

    def go(pair):
        start_remote(pair[0])
        start_remote(pair[1])

    def arrived(pair):
        finish_of(pair[0])
        finish_of(pair[1])

    swap_part(0)
    spot(0)
    swap_part(1)
    for ch in range(1, depth // group):
        spot(ch)

    my_rows = lax.broadcasted_iota(jnp.int32, (own, ap), 0) + lane_group * own
    my_lanes = lax.broadcasted_iota(jnp.int32, (own, ap), 1)

    def rows_of(member):
        return pl.ds(pl.multiple_of(member * own, own), own)

    home = rows_of(lane_group)

    def window_copy(q, o, spot_rows):
        return remote(
            pack.at[o, places_of(PARTS[q])],
            win.at[places_of(PARTS[q]), :, spot_rows, :],
            win_send.at[q, o],
            win_recv.at[q, o],
            half * 8 + peer(o),
            slab,
        )

    finish_of(loads[0])
    finish_of(loads[1])
    def pack_part(q):
        part = PARTS[q]
        for copy in swaps[q]:
            finish_of(copy)

        def fill(p, carry):
            d = plane_of(part, p)
            t = 2 * part[0] + p
            for i in range(2):
                low = raw[0, i, d]
                high = raw[1, i, d]
                for o in range(8):
                    member = half * 8 + (peer(o) if o < 7 else lane_group)
                    keep_row = my_rows >= anchors[0, member]
                    keep_col = my_lanes >= anchors[1, member]
                    a = jnp.where(keep_col, low[:, :ap], low[:, ap:])
                    b = jnp.where(keep_col, high[:, :ap], high[:, ap:])
                    value = jnp.where(keep_row, a, b)
                    if o < 7:
                        pack[o, t, i] = value
                    else:
                        win[t, i, home, :] = value
            return carry

        lax.fori_loop(0, 2 * (part[1] - part[0]), fill, 0)

    def send_part(q):
        for o in range(7):
            copy = window_copy(q, o, home)
            copy.start()
            due.append(((q, o, "sent"), copy.wait_send))
            landing = window_copy(q, o, rows_of(origin(o)))
            due.append(((q, o), landing.wait_recv))

    def sent_part(q):
        for o in range(7):
            finish_of((q, o, "sent"))

    row_anchor = anchors[0, shot]
    col_anchor = anchors[1, shot]

    def unwind(values, lane_shift, first_row):
        for t, x in enumerate(values):
            x = pltpu.roll(x, lane_shift, axis=1)
            tmp[t, :ap, :] = x
            tmp[t, ap:, :] = x
        return [tmp[t, pl.ds(first_row, ap), :] for t in range(len(values))]

    lane_back = (ap - col_anchor) % ap

    def settle(q):
        low, high = PARTS[q]
        width = high - low
        for o in range(7):
            finish_of((q, o))

        def one(p, carry):
            t = 2 * low + p
            values = [win[t, 0], win[t, 1], win[t + width, 0], win[t + width, 1]]
            values = unwind(values, lane_back, row_anchor)
            products = []
            for e in range(2):
                d = low + p if e == 0 else depth - high + p
                products.append(values[2 * e + 1] * ab[1, d])
            for e in range(2):
                d = low + p if e == 0 else depth - high + p
                bz[d + 1, inner, :] = values[2 * e]
                kp[d] = values[2 * e + 1]
                wb[0, d + 1, inner, :] = products[e]
            return carry

        lax.fori_loop(0, width, one, 0)

    def each(low, high, step):
        pairs = 2 if (high - low) % 2 == 0 else 1

        def some(i, carry):
            layers = []
            for t in range(pairs):
                d = low + i * pairs + t
                layers += [d, depth - 1 - d]
            for c0 in range(0, ap, CHUNK):
                stores = [step(d, c0) for d in layers]
                for store in stores:
                    store()
            return carry

        lax.fori_loop(0, (high - low) // pairs, some, 0)

    def coefficients(d, c0):
        first = (slab == 0) & (d == 0)
        last = (slab == slabs - 1) & (d == depth - 1)
        rows = lax.broadcasted_iota(jnp.int32, (CHUNK, ap), 0) + c0
        lanes = lax.broadcasted_iota(jnp.int32, (CHUNK, ap), 1)
        at = slice(PAD + c0, PAD + c0 + CHUNK)
        x = bz[d + 1, at, :]
        prev = bz[d + 1, PAD + c0 - 1 : PAD + c0 - 1 + CHUNK, :]
        succ = bz[d + 1, PAD + c0 + 1 : PAD + c0 + 1 + CHUNK, :]
        across = 0.5 * (x + prev)
        total = across + 0.5 * (x + succ)
        across = jnp.where(rows == 0, 0.0, across)
        prev = jnp.where(lanes == 0, 0.0, pltpu.roll(x, 1, axis=1))
        succ = jnp.where(lanes == ap - 1, 0.0, pltpu.roll(x, ap - 1, axis=1))
        along = 0.5 * (x + prev)
        total = total + along + 0.5 * (x + succ)
        along = jnp.where(lanes == 0, 0.0, along)
        low = 0.5 * (x + jnp.where(first, 0.0, bz[d, at, :]))
        high = 0.5 * (x + jnp.where(last, 0.0, bz[d + 2, at, :]))
        total = total + low + high
        low = jnp.where(first, 0.0, low)
        high = jnp.where(last, 0.0, high)

        def store():
            cr[d, at, :] = across
            cc[d, c0 : c0 + CHUNK, :] = along
            fd[d, c0 : c0 + CHUNK, :] = low
            fd[d + 1, c0 : c0 + CHUNK, :] = high
            dg[d, c0 : c0 + CHUNK, :] = total

        return store

    def spread(field, d, c0):
        at = PAD + c0
        x = field[d + 1, at : at + CHUNK, :]
        across = cc[d, c0 : c0 + CHUNK, :]
        sides = across * pltpu.roll(x, 1, axis=1)
        sides = sides + pltpu.roll(across * x, ap - 1, axis=1)
        total = fd[d, c0 : c0 + CHUNK, :] * field[d, at : at + CHUNK, :]
        total = total + fd[d + 1, c0 : c0 + CHUNK, :] * field[d + 2, at : at + CHUNK, :]
        total = total + cr[d, at : at + CHUNK, :] * field[d + 1, at - 1 : at - 1 + CHUNK, :]
        total = total + cr[d, at + 1 : at + 1 + CHUNK, :] * field[d + 1, at + 1 : at + 1 + CHUNK, :]
        return (total - dg[d, c0 : c0 + CHUNK, :] * x) + sides, x

    def forward(n):
        def step(d, c0):
            rows = slice(c0, c0 + CHUNK)
            at = slice(PAD + c0, PAD + c0 + CHUNK)
            q, x = spread(pb.at[n + 1], d, c0)
            nxt = 2.0 * x - pb[n, d + 1, at, :] + wavelet[0, n] * sf[d, rows, :]
            nxt = nxt + kp[d, rows, :] * q

            def store():
                qb[n, d, rows, :] = q
                pb[n + 2, d + 1, at, :] = nxt

            return store

        return step

    def backward(n):
        m = NT - n

        def step(d, c0):
            rows = slice(c0, c0 + CHUNK)
            at = slice(PAD + c0, PAD + c0 + CHUNK)
            q, _ = spread(wb.at[m], d, c0)
            now = 2.0 * ab[m + 1, d, rows, :] - ab[m, d, rows, :]
            now = now + (kc[d, rows, :] * pb[n + 1, d + 1, at, :] - ob[n - 1, d, rows, :])
            now = now + q
            product = kp[d, rows, :] * now if n > 1 else None
            term = now * qb[n - 1, d, rows, :]
            if m > 0:
                term = gb[d, rows, :] + term

            def store():
                ab[m + 2, d, rows, :] = now
                if n > 1:
                    wb[m + 1, d + 1, at, :] = product
                gb[d, rows, :] = term

            return store

        return step

    def grad_copy(r, o, spot_rows):
        places = places_of(RETURNS[r])
        return remote(
            gc.at[places, spot_rows, :],
            gr.at[o, places],
            grad_send.at[r, o],
            grad_recv.at[r, o],
            half * 8 + peer(o),
            slab,
        )

    pieces = [[grad_copy(r, o, rows_of(peer(o))) for o in range(7)] for r in range(len(RETURNS))]
    merges = []
    for r, span in enumerate(RETURNS):
        places = places_of(span)
        merges.append(
            remote(
                acc.at[1 - half, places],
                pr.at[places],
                merge_send.at[r],
                merge_recv.at[r],
                partner,
                slab,
            )
        )

    def hand_in(r):
        low, high = RETURNS[r]
        width = high - low

        def wind(p, carry):
            values = unwind([gb[low + p], gb[depth - high + p]], col_anchor % ap, ap - row_anchor)
            gc[2 * low + p] = values[0]
            gc[2 * low + width + p] = values[1]
            return carry

        lax.fori_loop(0, width, wind, 0)
        for copy in pieces[r]:
            start_remote(copy)

    def collect(r):
        low, high = RETURNS[r]
        for copy in pieces[r]:
            finish_of(copy)

        def one(t, carry):
            sums = [jnp.zeros((own, ap), f32) for _ in range(4)]
            for o in range(8):
                value = gr[o, t] if o < 7 else gc[t, home, :]
                member = half * 8 + (origin(o) if o < 7 else lane_group)
                keep_row = my_rows >= anchors[0, member]
                keep_col = my_lanes >= anchors[1, member]
                top = jnp.where(keep_row, value, 0.0)
                bottom = jnp.where(keep_row, 0.0, value)
                sums[0] += jnp.where(keep_col, top, 0.0)
                sums[1] += jnp.where(keep_col, 0.0, top)
                sums[2] += jnp.where(keep_col, bottom, 0.0)
                sums[3] += jnp.where(keep_col, 0.0, bottom)
            acc[0, t, :, :ap] = sums[0]
            acc[0, t, :, ap:] = sums[1]
            acc[1, t, :, :ap] = sums[2]
            acc[1, t, :, ap:] = sums[3]
            return carry

        lax.fori_loop(2 * low, 2 * high, one, 0)
        start_remote(merges[r])

    def finish(r):
        low, high = RETURNS[r]
        width = high - low
        finish_of(merges[r])

        def one(p, carry):
            t = 2 * low + p
            sums = [pr[t] + acc[half, t], pr[t + width] + acc[half, t + width]]
            grad_out[low + p] = sums[0]
            grad_out[depth - high + p] = sums[1]
            return carry

        lax.fori_loop(0, width, one, 0)

    pack_part(0)
    send_part(0)
    swap_part(2)
    pack_part(1)
    send_part(1)
    swap_part(3)
    go(wave_halo[0])
    pack_part(2)
    send_part(2)
    for i in range(2, 6):
        finish_of(loads[i])
    settle(0)
    go(buoy_halo)
    pack_part(3)
    sent_part(1)
    send_part(3)
    arrived(wave_halo[0])
    settle(1)
    arrived(buoy_halo)
    each(0, 2, coefficients)
    each(0, 1, forward(0))
    go(wave_halo[1])
    each(1, 2, forward(0))
    go(back_halo[0])
    arrived(wave_halo[1])
    each(0, 1, forward(1))
    go(wave_halo[2])
    settle(2)
    each(2, 4, coefficients)
    each(2, 4, forward(0))
    each(1, 3, forward(1))
    arrived(wave_halo[2])
    each(0, 1, forward(2))
    go(wave_halo[3])
    each(1, 2, forward(2))
    settle(3)
    each(4, 8, coefficients)
    arrived(back_halo[0])
    arrived(wave_halo[3])
    each(0, 1, forward(3))
    each(0, 1, backward(4))
    go(back_halo[1])
    each(4, 8, forward(0))
    each(3, 4, forward(1))
    each(4, 8, forward(1))
    each(2, 4, forward(2))
    each(4, 8, forward(2))
    each(1, 2, forward(3))
    each(1, 2, backward(4))
    each(2, 8, forward(3))
    start_local(pltpu.make_async_copy(pb.at[NT, body, inner, :], wave_out.at[0, 0], out_sem.at[0]))
    start_local(pltpu.make_async_copy(pb.at[NT + 1, body, inner, :], wave_out.at[0, 1], out_sem.at[1]))
    arrived(back_halo[1])
    each(0, 1, backward(3))
    go(back_halo[2])
    each(2, 8, backward(4))
    each(2, 8, backward(3))
    each(3, 4, backward(2))
    each(4, 8, backward(2))
    each(4, 8, backward(1))
    hand_in(0)
    each(1, 2, backward(3))
    each(1, 3, backward(2))
    arrived(back_halo[2])
    each(0, 1, backward(2))
    go(back_halo[3])
    start_local(pltpu.make_async_copy(ab.at[NT], adjoint_out.at[0, 0], out_sem.at[2]))
    each(2, 4, backward(1))
    hand_in(1)
    each(1, 2, backward(1))
    hand_in(2)
    arrived(back_halo[3])
    each(0, 1, backward(1))
    hand_in(3)
    start_local(pltpu.make_async_copy(ab.at[NT + 1], adjoint_out.at[0, 1], out_sem.at[3]))
    collect(0)
    collect(1)
    collect(2)
    finish(0)
    collect(3)
    finish(1)
    finish(2)
    finish(3)
    for wait in sent:
        wait()
    for _, wait in due:
        wait()


def shards(
    kappa,
    buoyancy,
    anchors,
    wave_start,
    adjoint_start,
    wavelet,
    source_cell,
    receiver_cells,
    observed,
):
    depth, own, side = kappa.shape
    ap = wave_start.shape[3]
    count = receiver_cells.shape[1]
    parts = len(PARTS)
    f32 = jnp.float32
    any_space = pl.BlockSpec(memory_space=pl.ANY)
    smem = pl.BlockSpec(memory_space=pltpu.SMEM)
    vmem = pl.BlockSpec(memory_space=pltpu.VMEM)
    padded = (depth + 2, ap + 2 * PAD, ap)
    plain = (depth, ap, ap)
    return pl.pallas_call(
        kernel,
        out_shape=(
            pltpu.VMEM(kappa.shape, f32),
            pltpu.VMEM(wave_start.shape, f32),
            pltpu.VMEM(adjoint_start.shape, f32),
        ),
        in_specs=[smem, smem, smem, any_space, any_space, any_space, any_space, vmem, vmem],
        out_specs=(vmem, any_space, any_space),
        scratch_shapes=[
            pltpu.VMEM((2, 2, depth, own, side), f32),
            pltpu.VMEM((7, depth, 2, own, ap), f32),
            pltpu.VMEM((depth, 2, ap, ap), f32),
            pltpu.VMEM((NT + 2,) + padded, f32),
            pltpu.VMEM((NT,) + plain, f32),
            pltpu.VMEM(plain, f32),
            pltpu.VMEM(padded, f32),
            pltpu.VMEM((depth + 1, ap, ap), f32),
            pltpu.VMEM((depth, ap + 2 * PAD, ap), f32),
            pltpu.VMEM(plain, f32),
            pltpu.VMEM(plain, f32),
            pltpu.VMEM((NT,) + padded, f32),
            pltpu.VMEM((NT + 2,) + plain, f32),
            pltpu.VMEM(plain, f32),
            pltpu.VMEM((NT,) + plain, f32),
            pltpu.VMEM(plain, f32),
            pltpu.VMEM((count, 13 * ap), jnp.bfloat16),
            pltpu.VMEM(plain, f32),
            pltpu.VMEM(plain, f32),
            pltpu.VMEM((7, depth, own, ap), f32),
            pltpu.VMEM((2, depth, own, side), f32),
            pltpu.VMEM((depth, own, side), f32),
            pltpu.VMEM((4, 2 * ap, ap), f32),
            pltpu.SemaphoreType.DMA((6,)),
            pltpu.SemaphoreType.DMA((parts, 2, 2)),
            pltpu.SemaphoreType.DMA((parts, 2, 2)),
            pltpu.SemaphoreType.DMA((parts, 7)),
            pltpu.SemaphoreType.DMA((parts, 7)),
            pltpu.SemaphoreType.DMA((2 * NT + 1, 2)),
            pltpu.SemaphoreType.DMA((2 * NT + 1, 2)),
            pltpu.SemaphoreType.DMA((len(RETURNS), 7)),
            pltpu.SemaphoreType.DMA((len(RETURNS), 7)),
            pltpu.SemaphoreType.DMA((len(RETURNS),)),
            pltpu.SemaphoreType.DMA((len(RETURNS),)),
            pltpu.SemaphoreType.DMA((4,)),
        ],
        compiler_params=pltpu.CompilerParams(
            collective_id=0, has_side_effects=True, vmem_limit_bytes=57 * 1024 * 1024
        ),
    )(
        anchors.T,
        wavelet,
        source_cell,
        kappa,
        buoyancy,
        wave_start,
        adjoint_start,
        jnp.transpose(receiver_cells, (2, 0, 1)),
        observed[0],
    )
def solution(mesh):
    in_specs = (
        P("slab", "shot", None),
        P("slab", "shot", None),
        P(),
        P("shot", None, "slab", None, None),
        P("shot", None, "slab", None, None),
        P("shot", None),
        P("shot", None),
        P("shot", None, None),
        P("shot", None, None),
    )
    out_specs = (
        P("slab", "shot", None),
        P("shot", None, "slab", None, None),
        P("shot", None, "slab", None, None),
    )
    return jax.shard_map(shards, mesh=mesh, in_specs=in_specs, out_specs=out_specs, check_vma=False)
```

```python
import jax
import jax.numpy as jnp
from jax import lax
from jax.experimental import pallas as pl
from jax.experimental.pallas import tpu as pltpu
from jax.sharding import PartitionSpec as P

MESH = pl.DeviceIdType.MESH
NT = 4
PAD = 8
CHUNK = 128
PARTS = ((0, 1), (1, 3), (3, 5), (5, 8))
RETURNS = ((4, 8), (2, 4), (1, 2), (0, 1))
OFFSETS = ((2, 0), (2, 1), (1, 0), (3, 0), (1, 1), (3, 1), (0, 1))


def kernel(
    anchors,
    wavelet,
    source,
    kappa,
    buoyancy,
    wave,
    adjoint,
    cells,
    observed,
    grad_out,
    wave_out,
    adjoint_out,
    raw,
    pack,
    win,
    pb,
    qb,
    kp,
    bz,
    fd,
    cr,
    cc,
    dg,
    wb,
    ab,
    kc,
    ob,
    sf,
    vb,
    gb,
    gc,
    gr,
    acc,
    pr,
    tmp,
    load_sem,
    swap_send,
    swap_recv,
    win_send,
    win_recv,
    halo_send,
    halo_recv,
    grad_send,
    grad_recv,
    merge_send,
    merge_recv,
    out_sem,
):
    depth, own, side = kappa.shape
    ap = side // 2
    f32 = jnp.float32
    shot = lax.axis_index("shot")
    slab = lax.axis_index("slab")
    slabs = lax.axis_size("slab")
    half = shot // 8
    lane_group = shot % 8
    px = lane_group // 2
    pc = lane_group % 2
    partner = (shot + 8) % 16
    below = (slab + 1) % slabs
    above = (slab + slabs - 1) % slabs

    def peer(o):
        dx, dc = OFFSETS[o]
        return ((px + dx) % 4) * 2 + (pc + dc) % 2

    def origin(o):
        dx, dc = OFFSETS[o]
        return ((px + 4 - dx) % 4) * 2 + (pc + 2 - dc) % 2

    sent = []
    due = []

    def start_local(copy):
        copy.start()
        due.append((copy, copy.wait))

    def start_remote(copy):
        copy.start()
        sent.append(copy.wait_send)
        due.append((copy, copy.wait_recv))

    def finish_of(copy):
        for i, (known, wait) in enumerate(due):
            if known is copy or (isinstance(copy, tuple) and known == copy):
                due.pop(i)
                wait()
                return
        raise ValueError(copy)

    def remote(src, dst, send, recv, to_shot, to_slab):
        return pltpu.make_async_remote_copy(
            src_ref=src,
            dst_ref=dst,
            send_sem=send,
            recv_sem=recv,
            device_id={"shot": to_shot, "slab": to_slab},
            device_id_type=MESH,
        )

    inner = pl.ds(PAD, ap)
    body = pl.ds(1, depth)

    barrier = pltpu.get_barrier_semaphore()

    def greet(to_shot, to_slab):
        pl.semaphore_signal(
            barrier, inc=1, device_id={"shot": to_shot, "slab": to_slab}, device_id_type=MESH
        )

    greet(partner, slab)
    greet(shot, below)
    greet(shot, above)
    for o in range(7):
        greet(half * 8 + peer(o), slab)

    loads = [
        pltpu.make_async_copy(buoyancy, raw.at[half, 0], load_sem.at[0]),
        pltpu.make_async_copy(kappa, raw.at[half, 1], load_sem.at[1]),
        pltpu.make_async_copy(wave.at[0, 0], pb.at[0, body, inner, :], load_sem.at[2]),
        pltpu.make_async_copy(wave.at[0, 1], pb.at[1, body, inner, :], load_sem.at[3]),
        pltpu.make_async_copy(adjoint.at[0, 0], ab.at[0], load_sem.at[4]),
        pltpu.make_async_copy(adjoint.at[0, 1], ab.at[1], load_sem.at[5]),
    ]
    for copy in loads:
        start_local(copy)

    margin = jnp.zeros((PAD, ap), f32)

    def clear(i, carry):
        for n in range(NT):
            pb[n + 1, i + 1, :PAD, :] = margin
            pb[n + 1, i + 1, PAD + ap :, :] = margin
            wb[n, i + 1, :PAD, :] = margin
            wb[n, i + 1, PAD + ap :, :] = margin
        bz[i + 1, :PAD, :] = margin
        bz[i + 1, PAD + ap :, :] = margin
        cr[i, PAD + ap :, :] = margin
        return carry

    lax.fori_loop(0, depth, clear, 0)

    count = cells.shape[2]
    rows_at = lax.broadcasted_iota(jnp.int32, (ap, ap), 0)
    lanes_at = lax.broadcasted_iota(jnp.int32, (ap, ap), 1)
    flat = (cells[0] - slab * depth) * ap + cells[1]
    upright = jnp.concatenate(
        [cells[2].astype(f32), observed[...], jnp.zeros((7 - NT, count), f32)], axis=0
    ).T
    hit = lax.broadcasted_iota(jnp.int32, (count, ap), 1).astype(f32) == upright[:, :1]

    for n in range(NT):
        rest = jnp.where(hit, upright[:, n + 1 : n + 2], 0.0)
        base = (n // 2) * 6 * ap + (n % 2) * ap
        for part in range(3):
            top = rest.astype(jnp.bfloat16)
            vb[:, base + part * 2 * ap : base + (part * 2 + 1) * ap] = top
            rest = rest - top.astype(f32)
    vb[:, 12 * ap :] = jnp.where(hit, 1.0, 0.0).astype(jnp.bfloat16)

    def mark(d, carry):
        here = (rows_at == source[0, 1]) & (lanes_at == source[0, 2])
        deep = jnp.where(source[0, 0] == slab * depth + d, 1.0, 0.0)
        sf[d, :, :] = jnp.where(here, deep, 0.0)
        return carry

    lax.fori_loop(0, depth, mark, 0)

    group = 4

    def spot(ch):
        at = lax.broadcasted_iota(jnp.int32, (group * ap, count), 0) + ch * (group * ap)
        onehot = jnp.where(flat == at, 1.0, 0.0).astype(jnp.bfloat16)

        def times(row, width):
            return lax.dot_general(
                onehot, vb[:, row : row + width], (((1,), (0,)), ((), ())), preferred_element_type=f32
            )

        for pair in range(NT // 2):
            total = times(pair * 6 * ap, 2 * ap)
            total = total + times(pair * 6 * ap + 2 * ap, 2 * ap)
            total = total + times(pair * 6 * ap + 4 * ap, 2 * ap)
            total = total.reshape(group, ap, 2 * ap)
            ob[2 * pair, pl.ds(ch * group, group), :, :] = total[:, :, :ap]
            ob[2 * pair + 1, pl.ds(ch * group, group), :, :] = total[:, :, ap:]
        kc[pl.ds(ch * group, group), :, :] = times(12 * ap, ap).reshape(group, ap, ap)

    pl.semaphore_wait(barrier, 10)

    def plane_of(span, p):
        low, high = span
        width = high - low
        return low + p + (p // width) * (depth - high - low - width)

    def places_of(span):
        low, high = span
        return pl.ds(2 * low, 2 * (high - low))

    swaps = []
    for q, (low, high) in enumerate(PARTS):
        swaps.append([])
        for i, ref in enumerate((buoyancy, kappa)):
            for e in range(2):
                planes = pl.ds(low if e == 0 else depth - high, high - low)
                swaps[q].append(
                    remote(
                        ref.at[planes],
                        raw.at[half, i, planes],
                        swap_send.at[q, i, e],
                        swap_recv.at[q, i, e],
                        partner,
                        slab,
                    )
                )

    def swap_part(q):
        for copy in swaps[q]:
            start_remote(copy)

    def field_halo(slot, field, src=None):
        first = field.at[1, inner, :] if src is None else src.at[0]
        last = field.at[depth, inner, :] if src is None else src.at[depth - 1]
        return (
            remote(
                first,
                field.at[depth + 1, inner, :],
                halo_send.at[slot, 0],
                halo_recv.at[slot, 0],
                shot,
                above,
            ),
            remote(
                last,
                field.at[0, inner, :],
                halo_send.at[slot, 1],
                halo_recv.at[slot, 1],
                shot,
                below,
            ),
        )

    wave_halo = [field_halo(0, pb.at[1], wave.at[0, 1])]
    wave_halo += [field_halo(n, pb.at[n + 1]) for n in range(1, NT)]
    back_halo = [field_halo(NT + m, wb.at[m]) for m in range(NT)]
    buoy_halo = field_halo(2 * NT, bz)

    def go(pair):
        start_remote(pair[0])
        start_remote(pair[1])

    def arrived(pair):
        finish_of(pair[0])
        finish_of(pair[1])

    swap_part(0)
    spot(0)
    swap_part(1)
    for ch in range(1, depth // group):
        spot(ch)

    my_rows = lax.broadcasted_iota(jnp.int32, (own, ap), 0) + lane_group * own
    my_lanes = lax.broadcasted_iota(jnp.int32, (own, ap), 1)

    def rows_of(member):
        return pl.ds(pl.multiple_of(member * own, own), own)

    home = rows_of(lane_group)

    def window_copy(q, o, spot_rows):
        return remote(
            pack.at[o, places_of(PARTS[q])],
            win.at[places_of(PARTS[q]), :, spot_rows, :],
            win_send.at[q, o],
            win_recv.at[q, o],
            half * 8 + peer(o),
            slab,
        )

    finish_of(loads[0])
    finish_of(loads[1])
    def pack_part(q):
        part = PARTS[q]
        for copy in swaps[q]:
            finish_of(copy)

        def fill(p, carry):
            d = plane_of(part, p)
            t = 2 * part[0] + p
            for i in range(2):
                low = raw[0, i, d]
                high = raw[1, i, d]
                for o in range(8):
                    member = half * 8 + (peer(o) if o < 7 else lane_group)
                    keep_row = my_rows >= anchors[0, member]
                    keep_col = my_lanes >= anchors[1, member]
                    a = jnp.where(keep_col, low[:, :ap], low[:, ap:])
                    b = jnp.where(keep_col, high[:, :ap], high[:, ap:])
                    value = jnp.where(keep_row, a, b)
                    if o < 7:
                        pack[o, t, i] = value
                    else:
                        win[t, i, home, :] = value
            return carry

        lax.fori_loop(0, 2 * (part[1] - part[0]), fill, 0)

    def send_part(q):
        for o in range(7):
            copy = window_copy(q, o, home)
            copy.start()
            due.append(((q, o, "sent"), copy.wait_send))
            landing = window_copy(q, o, rows_of(origin(o)))
            due.append(((q, o), landing.wait_recv))

    def sent_part(q):
        for o in range(7):
            finish_of((q, o, "sent"))

    row_anchor = anchors[0, shot]
    col_anchor = anchors[1, shot]

    def unwind(values, lane_shift, first_row):
        for t, x in enumerate(values):
            x = pltpu.roll(x, lane_shift, axis=1)
            tmp[t, :ap, :] = x
            tmp[t, ap:, :] = x
        return [tmp[t, pl.ds(first_row, ap), :] for t in range(len(values))]

    lane_back = (ap - col_anchor) % ap

    def settle(q):
        low, high = PARTS[q]
        width = high - low
        for o in range(7):
            finish_of((q, o))

        def one(p, carry):
            t = 2 * low + p
            values = [win[t, 0], win[t, 1], win[t + width, 0], win[t + width, 1]]
            values = unwind(values, lane_back, row_anchor)
            products = []
            for e in range(2):
                d = low + p if e == 0 else depth - high + p
                products.append(values[2 * e + 1] * ab[1, d])
            for e in range(2):
                d = low + p if e == 0 else depth - high + p
                bz[d + 1, inner, :] = values[2 * e]
                kp[d] = values[2 * e + 1]
                wb[0, d + 1, inner, :] = products[e]
            return carry

        lax.fori_loop(0, width, one, 0)

    def each(low, high, step):
        pairs = 2 if (high - low) % 2 == 0 else 1

        def some(i, carry):
            layers = []
            for t in range(pairs):
                d = low + i * pairs + t
                layers += [d, depth - 1 - d]
            for c0 in range(0, ap, CHUNK):
                stores = [step(d, c0) for d in layers]
                for store in stores:
                    store()
            return carry

        lax.fori_loop(0, (high - low) // pairs, some, 0)

    def coefficients(d, c0):
        first = (slab == 0) & (d == 0)
        last = (slab == slabs - 1) & (d == depth - 1)
        rows = lax.broadcasted_iota(jnp.int32, (CHUNK, ap), 0) + c0
        lanes = lax.broadcasted_iota(jnp.int32, (CHUNK, ap), 1)
        at = slice(PAD + c0, PAD + c0 + CHUNK)
        x = bz[d + 1, at, :]
        prev = bz[d + 1, PAD + c0 - 1 : PAD + c0 - 1 + CHUNK, :]
        succ = bz[d + 1, PAD + c0 + 1 : PAD + c0 + 1 + CHUNK, :]
        across = 0.5 * (x + prev)
        total = across + 0.5 * (x + succ)
        across = jnp.where(rows == 0, 0.0, across)
        prev = jnp.where(lanes == 0, 0.0, pltpu.roll(x, 1, axis=1))
        succ = jnp.where(lanes == ap - 1, 0.0, pltpu.roll(x, ap - 1, axis=1))
        along = 0.5 * (x + prev)
        total = total + along + 0.5 * (x + succ)
        along = jnp.where(lanes == 0, 0.0, along)
        low = 0.5 * (x + jnp.where(first, 0.0, bz[d, at, :]))
        high = 0.5 * (x + jnp.where(last, 0.0, bz[d + 2, at, :]))
        total = total + low + high
        low = jnp.where(first, 0.0, low)
        high = jnp.where(last, 0.0, high)

        def store():
            cr[d, at, :] = across
            cc[d, c0 : c0 + CHUNK, :] = along
            fd[d, c0 : c0 + CHUNK, :] = low
            fd[d + 1, c0 : c0 + CHUNK, :] = high
            dg[d, c0 : c0 + CHUNK, :] = total

        return store

    def spread(field, d, c0):
        at = PAD + c0
        x = field[d + 1, at : at + CHUNK, :]
        across = cc[d, c0 : c0 + CHUNK, :]
        sides = across * pltpu.roll(x, 1, axis=1)
        sides = sides + pltpu.roll(across * x, ap - 1, axis=1)
        total = fd[d, c0 : c0 + CHUNK, :] * field[d, at : at + CHUNK, :]
        total = total + fd[d + 1, c0 : c0 + CHUNK, :] * field[d + 2, at : at + CHUNK, :]
        total = total + cr[d, at : at + CHUNK, :] * field[d + 1, at - 1 : at - 1 + CHUNK, :]
        total = total + cr[d, at + 1 : at + 1 + CHUNK, :] * field[d + 1, at + 1 : at + 1 + CHUNK, :]
        return (total - dg[d, c0 : c0 + CHUNK, :] * x) + sides, x

    def forward(n):
        def step(d, c0):
            rows = slice(c0, c0 + CHUNK)
            at = slice(PAD + c0, PAD + c0 + CHUNK)
            q, x = spread(pb.at[n + 1], d, c0)
            nxt = 2.0 * x - pb[n, d + 1, at, :] + wavelet[0, n] * sf[d, rows, :]
            nxt = nxt + kp[d, rows, :] * q

            def store():
                qb[n, d, rows, :] = q
                pb[n + 2, d + 1, at, :] = nxt

            return store

        return step

    def backward(n):
        m = NT - n

        def step(d, c0):
            rows = slice(c0, c0 + CHUNK)
            at = slice(PAD + c0, PAD + c0 + CHUNK)
            q, _ = spread(wb.at[m], d, c0)
            now = 2.0 * ab[m + 1, d, rows, :] - ab[m, d, rows, :]
            now = now + (kc[d, rows, :] * pb[n + 1, d + 1, at, :] - ob[n - 1, d, rows, :])
            now = now + q
            product = kp[d, rows, :] * now if n > 1 else None
            term = now * qb[n - 1, d, rows, :]
            if m > 0:
                term = gb[d, rows, :] + term

            def store():
                ab[m + 2, d, rows, :] = now
                if n > 1:
                    wb[m + 1, d + 1, at, :] = product
                gb[d, rows, :] = term

            return store

        return step

    def grad_copy(r, o, spot_rows):
        places = places_of(RETURNS[r])
        return remote(
            gc.at[places, spot_rows, :],
            gr.at[o, places],
            grad_send.at[r, o],
            grad_recv.at[r, o],
            half * 8 + peer(o),
            slab,
        )

    pieces = [[grad_copy(r, o, rows_of(peer(o))) for o in range(7)] for r in range(len(RETURNS))]
    merges = []
    for r, span in enumerate(RETURNS):
        places = places_of(span)
        merges.append(
            remote(
                acc.at[1 - half, places],
                pr.at[places],
                merge_send.at[r],
                merge_recv.at[r],
                partner,
                slab,
            )
        )

    def hand_in(r):
        low, high = RETURNS[r]
        width = high - low

        def wind(p, carry):
            values = unwind([gb[low + p], gb[depth - high + p]], col_anchor % ap, ap - row_anchor)
            gc[2 * low + p] = values[0]
            gc[2 * low + width + p] = values[1]
            return carry

        lax.fori_loop(0, width, wind, 0)
        for copy in pieces[r]:
            start_remote(copy)

    def collect(r):
        low, high = RETURNS[r]
        for copy in pieces[r]:
            finish_of(copy)

        def one(t, carry):
            sums = [jnp.zeros((own, ap), f32) for _ in range(4)]
            for o in range(8):
                value = gr[o, t] if o < 7 else gc[t, home, :]
                member = half * 8 + (origin(o) if o < 7 else lane_group)
                keep_row = my_rows >= anchors[0, member]
                keep_col = my_lanes >= anchors[1, member]
                top = jnp.where(keep_row, value, 0.0)
                bottom = jnp.where(keep_row, 0.0, value)
                sums[0] += jnp.where(keep_col, top, 0.0)
                sums[1] += jnp.where(keep_col, 0.0, top)
                sums[2] += jnp.where(keep_col, bottom, 0.0)
                sums[3] += jnp.where(keep_col, 0.0, bottom)
            acc[0, t, :, :ap] = sums[0]
            acc[0, t, :, ap:] = sums[1]
            acc[1, t, :, :ap] = sums[2]
            acc[1, t, :, ap:] = sums[3]
            return carry

        lax.fori_loop(2 * low, 2 * high, one, 0)
        start_remote(merges[r])

    def finish(r):
        low, high = RETURNS[r]
        width = high - low
        finish_of(merges[r])

        def one(p, carry):
            t = 2 * low + p
            sums = [pr[t] + acc[half, t], pr[t + width] + acc[half, t + width]]
            grad_out[low + p] = sums[0]
            grad_out[depth - high + p] = sums[1]
            return carry

        lax.fori_loop(0, width, one, 0)

    pack_part(0)
    send_part(0)
    swap_part(2)
    pack_part(1)
    send_part(1)
    swap_part(3)
    go(wave_halo[0])
    pack_part(2)
    send_part(2)
    for i in range(2, 6):
        finish_of(loads[i])
    settle(0)
    go(buoy_halo)
    pack_part(3)
    send_part(3)
    arrived(wave_halo[0])
    settle(1)
    arrived(buoy_halo)
    each(0, 2, coefficients)
    each(0, 1, forward(0))
    go(wave_halo[1])
    each(1, 2, forward(0))
    go(back_halo[0])
    arrived(wave_halo[1])
    each(0, 1, forward(1))
    go(wave_halo[2])
    settle(2)
    each(2, 4, coefficients)
    each(2, 4, forward(0))
    each(1, 3, forward(1))
    arrived(wave_halo[2])
    each(0, 1, forward(2))
    go(wave_halo[3])
    each(1, 2, forward(2))
    settle(3)
    each(4, 8, coefficients)
    arrived(back_halo[0])
    arrived(wave_halo[3])
    each(0, 1, forward(3))
    each(0, 1, backward(4))
    go(back_halo[1])
    each(4, 8, forward(0))
    each(3, 4, forward(1))
    each(4, 8, forward(1))
    each(2, 4, forward(2))
    each(4, 8, forward(2))
    each(1, 2, forward(3))
    each(1, 2, backward(4))
    each(2, 8, forward(3))
    start_local(pltpu.make_async_copy(pb.at[NT, body, inner, :], wave_out.at[0, 0], out_sem.at[0]))
    start_local(pltpu.make_async_copy(pb.at[NT + 1, body, inner, :], wave_out.at[0, 1], out_sem.at[1]))
    arrived(back_halo[1])
    each(0, 1, backward(3))
    go(back_halo[2])
    each(2, 8, backward(4))
    each(2, 8, backward(3))
    each(3, 4, backward(2))
    each(4, 8, backward(2))
    each(4, 8, backward(1))
    hand_in(0)
    each(1, 2, backward(3))
    each(1, 3, backward(2))
    arrived(back_halo[2])
    each(0, 1, backward(2))
    go(back_halo[3])
    start_local(pltpu.make_async_copy(ab.at[NT], adjoint_out.at[0, 0], out_sem.at[2]))
    each(2, 4, backward(1))
    hand_in(1)
    each(1, 2, backward(1))
    hand_in(2)
    arrived(back_halo[3])
    each(0, 1, backward(1))
    hand_in(3)
    start_local(pltpu.make_async_copy(ab.at[NT + 1], adjoint_out.at[0, 1], out_sem.at[3]))
    collect(0)
    collect(1)
    collect(2)
    finish(0)
    collect(3)
    finish(1)
    finish(2)
    finish(3)
    for wait in sent:
        wait()
    for _, wait in due:
        wait()


def shards(
    kappa,
    buoyancy,
    anchors,
    wave_start,
    adjoint_start,
    wavelet,
    source_cell,
    receiver_cells,
    observed,
):
    depth, own, side = kappa.shape
    ap = wave_start.shape[3]
    count = receiver_cells.shape[1]
    parts = len(PARTS)
    f32 = jnp.float32
    any_space = pl.BlockSpec(memory_space=pl.ANY)
    smem = pl.BlockSpec(memory_space=pltpu.SMEM)
    vmem = pl.BlockSpec(memory_space=pltpu.VMEM)
    padded = (depth + 2, ap + 2 * PAD, ap)
    plain = (depth, ap, ap)
    return pl.pallas_call(
        kernel,
        out_shape=(
            pltpu.VMEM(kappa.shape, f32),
            pltpu.VMEM(wave_start.shape, f32),
            pltpu.VMEM(adjoint_start.shape, f32),
        ),
        in_specs=[smem, smem, smem, any_space, any_space, any_space, any_space, vmem, vmem],
        out_specs=(vmem, any_space, any_space),
        scratch_shapes=[
            pltpu.VMEM((2, 2, depth, own, side), f32),
            pltpu.VMEM((7, depth, 2, own, ap), f32),
            pltpu.VMEM((depth, 2, ap, ap), f32),
            pltpu.VMEM((NT + 2,) + padded, f32),
            pltpu.VMEM((NT,) + plain, f32),
            pltpu.VMEM(plain, f32),
            pltpu.VMEM(padded, f32),
            pltpu.VMEM((depth + 1, ap, ap), f32),
            pltpu.VMEM((depth, ap + 2 * PAD, ap), f32),
            pltpu.VMEM(plain, f32),
            pltpu.VMEM(plain, f32),
            pltpu.VMEM((NT,) + padded, f32),
            pltpu.VMEM((NT + 2,) + plain, f32),
            pltpu.VMEM(plain, f32),
            pltpu.VMEM((NT,) + plain, f32),
            pltpu.VMEM(plain, f32),
            pltpu.VMEM((count, 13 * ap), jnp.bfloat16),
            pltpu.VMEM(plain, f32),
            pltpu.VMEM(plain, f32),
            pltpu.VMEM((7, depth, own, ap), f32),
            pltpu.VMEM((2, depth, own, side), f32),
            pltpu.VMEM((depth, own, side), f32),
            pltpu.VMEM((4, 2 * ap, ap), f32),
            pltpu.SemaphoreType.DMA((6,)),
            pltpu.SemaphoreType.DMA((parts, 2, 2)),
            pltpu.SemaphoreType.DMA((parts, 2, 2)),
            pltpu.SemaphoreType.DMA((parts, 7)),
            pltpu.SemaphoreType.DMA((parts, 7)),
            pltpu.SemaphoreType.DMA((2 * NT + 1, 2)),
            pltpu.SemaphoreType.DMA((2 * NT + 1, 2)),
            pltpu.SemaphoreType.DMA((len(RETURNS), 7)),
            pltpu.SemaphoreType.DMA((len(RETURNS), 7)),
            pltpu.SemaphoreType.DMA((len(RETURNS),)),
            pltpu.SemaphoreType.DMA((len(RETURNS),)),
            pltpu.SemaphoreType.DMA((4,)),
        ],
        compiler_params=pltpu.CompilerParams(
            collective_id=0, has_side_effects=True, vmem_limit_bytes=57 * 1024 * 1024
        ),
    )(
        anchors.T,
        wavelet,
        source_cell,
        kappa,
        buoyancy,
        wave_start,
        adjoint_start,
        jnp.transpose(receiver_cells, (2, 0, 1)),
        observed[0],
    )
def solution(mesh):
    in_specs = (
        P("slab", "shot", None),
        P("slab", "shot", None),
        P(),
        P("shot", None, "slab", None, None),
        P("shot", None, "slab", None, None),
        P("shot", None),
        P("shot", None),
        P("shot", None, None),
        P("shot", None, None),
    )
    out_specs = (
        P("slab", "shot", None),
        P("shot", None, "slab", None, None),
        P("shot", None, "slab", None, None),
    )
    return jax.shard_map(shards, mesh=mesh, in_specs=in_specs, out_specs=out_specs, check_vma=False)
```
